32 devices in a mesh: det: 4 (over y, core), tm: 8 (over z, x).
Axes of the slice: x: 2, y: 2, z: 4, core: 2. Of those that a mesh axis runs over, the one named last changes fastest.
Arguments:
- detector_data: float32 [256, 65536], P('det', 'tm'), may hold values from -6 to 6
- sky_map: float32 [4096, 8192], P(('det', 'tm')), may hold values from -6 to 6
- pointing: int32 [256, 512], P('det', 'tm'), may hold values from 0 to 2047
- request_owner: int32 [512, 1], P(('det', 'tm')), may hold values from 0 to 7; in each aligned block of 16 rows (0 to 15, 16 to 31, ...) at most 4 rows name the same one
- request_block: int32 [512], P(('det', 'tm')), may hold values from 0 to 63
- beam_kernel: float32 [128, 128], replicated, may hold values from -0.5 to 0.5
- inv_white: float32 [256, 32], P('det'), may hold values from 0.5 to 4
- mode_loading: float32 [256, 16], P('det'), may hold values from -1.5 to 1.5
- mode_kernel: float32 [32, 16, 16], replicated, may hold values from -0.75 to 0.75
Outputs:
- map_gradient: float32 [4096, 8192], P(('det', 'tm'))
The draws below stay inside these ranges and needn't reach their ends.
Inputs may be any that keep to these rules, and one draw needn't show every extreme that they name: `request_owner`: among the 16 requests of one device, no owner is named more than 4 times, and in every draw some device names some owner exactly 4 times.
All inputs are finite; a program needn't handle non-finite values.
Results may differ from the reference program's by a relative error of at most 0.0003.
Values sent between devices are 32-bit elements; how exact they have to be, the bound alone decides.
A program may use at most 256 MiB of HBM per device.

```python
import math
import jax
import jax.numpy as jnp
import numpy as np
from jax import lax

DET_DEV = 64
SAMPLES = 8192
TILE = 128
MODES = 16
NBAND = 32
BANDW = 128
LIST = 16
NY = 4096
NX = 8192
NDET = 256
NSAMP = 65536
BROWS = 128
BPD = 64
CAP = 4
NTILE = 64
N_DET = 4
N_TM = 8
DEVICES = 32


def draw_sky_map(key, part):
    phase_key = jax.random.fold_in(key, 11)
    second_key = jax.random.fold_in(key, 12)
    noise_key = jax.random.fold_in(key, 13)
    row_index = jnp.arange(NY, dtype=jnp.int32)[:, None]
    first_turn = (row_index * 255 % 512).astype(jnp.float32) * (2.0 * math.pi / 512.0)
    second_turn = (row_index * 15 % 32).astype(jnp.float32) * (2.0 * math.pi / 32.0)
    first_phase = jax.random.uniform(phase_key, (1, NX), jnp.float32, -math.pi, math.pi)
    second_phase = jax.random.uniform(second_key, (1, NX), jnp.float32, -math.pi, math.pi)
    amplitudes = jnp.full((2, 1, NX), 3.0, jnp.float32)
    noise = 0.7 * jax.random.normal(noise_key, (NY, NX), jnp.float32)
    waves = amplitudes[0] * jnp.cos(first_turn + first_phase) + amplitudes[1] * jnp.cos(second_turn + second_phase)
    return jnp.clip(waves + noise, -6.0, 6.0).astype(jnp.float32)


def place_ends(array, rng, low, high):
    spot = [jax.random.randint(jax.random.fold_in(rng, axis), (), 0, length) for axis, length in enumerate(array.shape)]
    widest = array.shape.index(max(array.shape))
    next_to = spot[:widest] + [(spot[widest] + 1) % array.shape[widest]] + spot[widest + 1:]
    return array.at[tuple(spot)].set(low).at[tuple(next_to)].set(high)


def block_scale(key, shape, split, low, high):
    level, own = 1.0, jax.random.fold_in(key, 6)
    for axis_at, parts in split:
        draws = jnp.exp(jax.random.uniform(jax.random.fold_in(own, axis_at), (parts,), jnp.float32, low / len(split), high / len(split)))
        level = level * jnp.repeat(draws, shape[axis_at] // parts).reshape([-1 if axis == axis_at else 1 for axis in range(len(shape))])
    return level


def routed_block(rng, own, number, rows, amount, top, limit, slope):
    ranking = jax.random.permutation(rng, amount)
    crowded, ordinary = load_shares(amount, rows * top, limit, slope, True), load_shares(amount, rows * top, limit, slope, False)
    places = jnp.arange(amount)

    def named(lengths, rotation):
        used = int((lengths > 0).sum())
        fixed = max(1, used // 4)
        passed = fixed + (places - fixed + rotation * (used - fixed)) % max(1, amount - fixed)
        return jnp.zeros((amount,), jnp.int32).at[ranking[jnp.where(places < fixed, places, passed)]].set(jnp.asarray(lengths, jnp.int32))

    lengths = jnp.where(number % 4 == 0, named(crowded, number // 4), named(ordinary, number - number // 4 - 1))
    mixed = jax.random.permutation(jax.random.fold_in(own, 3), amount)
    giver, taker = mixed[0:amount // 2 * 2:2], mixed[1:amount // 2 * 2:2]
    margin = jnp.minimum(lengths[giver] - 1, limit - lengths[taker]) // 2
    margin = jnp.where((giver == ranking[0]) | (taker == ranking[0]) | (lengths[taker] == 0), 0, jnp.maximum(margin, 0))
    passed = jax.random.randint(jax.random.fold_in(own, 4), (amount // 2,), 0, 1 << 20) % (margin + 1)
    lengths = lengths.at[giver].add(-passed).at[taker].add(passed)
    items = jnp.searchsorted(jnp.cumsum(lengths), jnp.arange(rows * top), side="right").astype(jnp.int32)
    grid = items.reshape(top, rows).T
    grid = grid[jax.random.permutation(jax.random.fold_in(own, 1), rows)]
    rotation = jax.random.randint(jax.random.fold_in(own, 2), (rows, 1), 0, top)
    return jnp.take_along_axis(grid, (jnp.arange(top)[None, :] + rotation) % top, axis=1)


def load_shares(number_of, total, reach, slope, full):
    weights = [(1 << 20) // math.isqrt(rank ** slope) + 1 for rank in range(1, number_of + 1)]
    largest = reach if full else min(reach, max(-(-total // number_of), total * weights[0] // sum(weights)))
    least = 1 if total - largest >= number_of - 1 else 0
    counts, surplus = [largest] + [least] * (number_of - 1), total - largest - least * (number_of - 1)
    while surplus > 0:
        candidates = [i for i in range(1, number_of) if counts[i] < largest] or [i for i in range(1, number_of) if counts[i] < reach]
        pool, left = sum([weights[i] for i in candidates]), surplus
        for i in candidates:
            more = min(reach - counts[i], max(1, left * weights[i] // pool), surplus)
            counts[i] = counts[i] + more
            surplus = surplus - more
    return np.array(counts)


def scatter_about(key, dims, width, most, split=(), held_as=jnp.bfloat16):
    values = jax.random.normal(key, dims, jnp.float32) * width
    if len(split) > 0:
        values = block_scale(key, dims, split, -0.22, 0.18) * values
    return jnp.clip(values, min=-most, max=most).astype(held_as)


def setup_inputs(seed: int = 0) -> dict:
    seeds = jax.random.split(jax.random.key(seed), 10)
    detector_data = scatter_about(seeds[0], (NDET, NSAMP), 1.0, 6.0, ((0, 4), (1, 8)), jnp.float32)
    sky_map = draw_sky_map(jax.random.fold_in(seeds[9], 71), 0)
    pointing = place_ends(jax.random.randint(seeds[2], (NDET, NSAMP // TILE), 0, LIST * BROWS), jax.random.fold_in(seeds[2], 1), 0, (LIST * BROWS) - 1).astype(jnp.int32)
    request_owner_keys = jax.random.split(jax.random.fold_in(seeds[3], 1), (DEVICES * LIST) // LIST)
    request_owner_turns = jax.random.permutation(jax.random.fold_in(seeds[3], 3), (DEVICES * LIST) // LIST)
    request_owner = jax.vmap(lambda own, number: routed_block(jax.random.fold_in(seeds[3], 2), own, number, LIST, N_TM, 1, CAP, 2))(request_owner_keys, request_owner_turns).reshape((DEVICES * LIST, 1))
    request_block = place_ends(jax.random.randint(seeds[4], (DEVICES * LIST,), 0, BPD), jax.random.fold_in(seeds[4], 1), 0, BPD - 1).astype(jnp.int32)
    beam_kernel = scatter_about(seeds[5], (TILE, TILE), TILE ** -0.5, 0.5, (), jnp.float32)
    inv_white = jnp.clip(jnp.exp(math.log(4.0) - 2.0794415 * jax.random.uniform(seeds[6], (NDET, NBAND), jnp.float32) ** block_scale(seeds[6], (NDET, NBAND), ((0, 4),), -0.2, 0.2)), 0.5, 4.0)
    mode_loading = scatter_about(seeds[7], (NDET, MODES), (max(NDET // 16, 1)) ** -0.5, 1.5, ((0, 4),), jnp.float32)
    mode_kernel = scatter_about(seeds[8], (NBAND, MODES, MODES), (4 * MODES) ** -0.5, 0.75, (), jnp.float32)
    return {"detector_data": detector_data, "sky_map": sky_map, "pointing": pointing, "request_owner": request_owner, "request_block": request_block, "beam_kernel": beam_kernel, "inv_white": inv_white, "mode_loading": mode_loading, "mode_kernel": mode_kernel}


precise = lax.Precision.HIGHEST

def prior_gain(vertical, horizontal, total_rows, total_cols):
    fold_rows = jnp.minimum(vertical, total_rows - vertical).astype(jnp.float32) / total_rows
    fold_cols = jnp.minimum(horizontal, total_cols - horizontal).astype(jnp.float32) / total_cols
    radial_sq = fold_rows * fold_rows + fold_cols * fold_cols
    length_scale = total_rows / 64.0
    knee_sq = 1.0 / (2.0 * math.pi * length_scale) ** 2
    return 1.0 + radial_sq / 0.05 + 0.25 / jnp.sqrt(radial_sq + knee_sq)

def reference(detector_data, sky_map, pointing, request_owner, request_block, beam_kernel, inv_white, mode_loading, mode_kernel):
    sky_grid = sky_map.reshape(NY, BPD, TILE)
    owner_all = request_owner[:, 0].reshape(N_DET, N_TM, LIST)
    block_all = request_block.reshape(N_DET, N_TM, LIST)
    frequency = jnp.arange(SAMPLES, dtype=jnp.int32)
    folded = jnp.minimum(frequency, SAMPLES - frequency)
    band_index = jnp.minimum(folded // BANDW, NBAND - 1)
    weight_freq = inv_white[:, band_index]
    kernel_freq = mode_kernel[band_index]
    det_group = (jnp.arange(NDET, dtype=jnp.int32) // DET_DEV)[:, None]

    def per_segment(gradient_grid, segment):
        data_now = lax.dynamic_slice_in_dim(detector_data, segment * SAMPLES, SAMPLES, 1)
        tiles_now = lax.dynamic_slice_in_dim(pointing, segment * NTILE, NTILE, 1)
        list_slot = tiles_now // BROWS
        block_row = tiles_now % BROWS
        owner_tm = owner_all[det_group, segment, list_slot]
        block_col = block_all[det_group, segment, list_slot]
        map_row = (det_group * N_TM + owner_tm) * BROWS + block_row
        sky_rows = sky_grid[map_row, block_col]
        signal = jnp.einsum('jsp,ip->jsi', sky_rows, beam_kernel, precision=precise).reshape(NDET, SAMPLES)
        spectrum = jnp.fft.fft(data_now - signal, axis=1)
        spec_real = jnp.real(spectrum)
        spec_imag = jnp.imag(spectrum)
        proj_real = jnp.einsum('jm,jf->mf', mode_loading, weight_freq * spec_real, precision=precise)
        proj_imag = jnp.einsum('jm,jf->mf', mode_loading, weight_freq * spec_imag, precision=precise)
        coupled_real = jnp.einsum('fmn,nf->mf', kernel_freq, proj_real, precision=precise)
        coupled_imag = jnp.einsum('fmn,nf->mf', kernel_freq, proj_imag, precision=precise)
        filt_real = weight_freq * (spec_real - jnp.einsum('jm,mf->jf', mode_loading, coupled_real, precision=precise))
        filt_imag = weight_freq * (spec_imag - jnp.einsum('jm,mf->jf', mode_loading, coupled_imag, precision=precise))
        cleaned = jnp.real(jnp.fft.ifft(lax.complex(filt_real, filt_imag), axis=1))
        tile_grads = jnp.einsum('jsi,ip->jsp', cleaned.reshape(NDET, NTILE, TILE), beam_kernel, precision=precise)
        gradient_grid = gradient_grid.at[map_row, block_col].add(tile_grads)
        return (gradient_grid, None)
    start_grid = jnp.zeros((NY, BPD, TILE), jnp.float32)
    gradient_grid = lax.scan(per_segment, start_grid, jnp.arange(N_TM, dtype=jnp.int32))[0]
    map_spectrum = jnp.fft.fft2(sky_map)
    gain_grid = prior_gain(jnp.arange(NY, dtype=jnp.int32)[:, None], jnp.arange(NX, dtype=jnp.int32)[None, :], NY, NX)
    prior_term = jnp.real(jnp.fft.ifft2(map_spectrum * gain_grid))
    return gradient_grid.reshape(NY, NX) - prior_term
```

```python
import functools
import math

import jax
import jax.numpy as jnp
import ml_dtypes
import numpy as np
from jax import lax
from jax.experimental import pallas as pl
from jax.experimental.pallas import tpu as pltpu
from jax.sharding import PartitionSpec as P

BAND_WIDTH = 128
LANES = 128
LIMIT = 50 * 1024 * 1024
F32 = jnp.float32
BF16 = jnp.bfloat16


def group_frequencies(length):
    half = LANES // 2
    outer = length // LANES
    steps = np.arange(LANES)
    freq = np.zeros((outer // 2, 2 * LANES), np.int64)
    for group in range(1, outer // 2):
        freq[group] = np.concatenate([group + outer * steps] * 2)
    low = outer * np.concatenate([np.arange(half + 1), np.arange(1, half)])
    middle = outer // 2 + outer * np.concatenate([np.arange(half)] * 2)
    freq[0] = np.concatenate([low, middle])
    return freq


def group_tables(length):
    half = LANES // 2
    freq = group_frequencies(length)
    groups = freq.shape[0]
    steps = np.arange(LANES)
    forward = np.zeros((groups, 2 * LANES, 2 * LANES))
    weight = np.ones((groups, 2 * LANES))
    angle = 2.0 * math.pi / length
    for group in range(groups):
        turn = (steps[:, None] * freq[group][None, :] % length) * angle
        cosine, sine = np.cos(turn), np.sin(turn)
        if group > 0:
            forward[group, :LANES, :LANES] = cosine[:, :LANES]
            forward[group, LANES:, :LANES] = sine[:, :LANES]
            forward[group, :LANES, LANES:] = -sine[:, LANES:]
            forward[group, LANES:, LANES:] = cosine[:, LANES:]
        else:
            forward[0, :LANES, : half + 1] = cosine[:, : half + 1]
            forward[0, :LANES, half + 1 : LANES] = -sine[:, half + 1 : LANES]
            forward[0, LANES:, LANES : LANES + half] = cosine[:, LANES : LANES + half]
            forward[0, LANES:, LANES + half :] = -sine[:, LANES + half :]
            weight[0, :] = 2.0
            weight[0, 0] = 1.0
            weight[0, half] = 1.0
    backward = (forward * weight[:, None, :] / length).transpose(0, 2, 1)
    return forward, backward


def halves(table):
    high = table.astype(np.float32).astype(ml_dtypes.bfloat16)
    low = (table - high.astype(np.float64)).astype(ml_dtypes.bfloat16)
    return high, low


def split(value):
    high = value.astype(BF16)
    return high, (value - high.astype(F32)).astype(BF16)


def multiply(left, right, dims=(((1,), (0,)), ((), ()))):
    dot = functools.partial(lax.dot_general, dimension_numbers=dims, preferred_element_type=F32)
    return dot(left[0], right[0]) + (dot(left[1], right[0]) + dot(left[0], right[1]))


def forward_stage(load, start, step, count):
    if count == 2:
        first, second = load(start), load(start + step)
        return [(first + second, None), (first - second, None)]
    even = forward_stage(load, start, 2 * step, count // 2)
    odd = forward_stage(load, start + step, 2 * step, count // 2)
    out = [None] * (count // 2 + 1)
    out[0] = (even[0][0] + odd[0][0], None)
    out[count // 2] = (even[0][0] - odd[0][0], None)
    out[count // 4] = (even[count // 4][0], -odd[count // 4][0])
    for k in range(1, count // 4):
        cosine, sine = math.cos(2 * math.pi * k / count), math.sin(2 * math.pi * k / count)
        odd_re, odd_im = odd[k]
        turn_re = cosine * odd_re + sine * odd_im
        turn_im = cosine * odd_im - sine * odd_re
        out[k] = (even[k][0] + turn_re, even[k][1] + turn_im)
        out[count // 2 - k] = (even[k][0] - turn_re, turn_im - even[k][1])
    return out


def backward_stage(spec, store, start, step):
    count = 2 * (len(spec) - 1)
    if count == 2:
        store(start, spec[0][0] + spec[1][0])
        store(start + step, spec[0][0] - spec[1][0])
        return
    even, odd = [None] * (count // 4 + 1), [None] * (count // 4 + 1)
    even[0] = (spec[0][0] + spec[count // 2][0], None)
    odd[0] = (spec[0][0] - spec[count // 2][0], None)
    middle = spec[count // 4]
    even[count // 4] = (2.0 * middle[0], None)
    odd[count // 4] = (-2.0 * middle[1], None)
    for k in range(1, count // 4):
        cosine, sine = math.cos(2 * math.pi * k / count), math.sin(2 * math.pi * k / count)
        (a_re, a_im), (b_re, b_im) = spec[k], spec[count // 2 - k]
        even[k] = (a_re + b_re, a_im - b_im)
        diff_re, diff_im = a_re - b_re, a_im + b_im
        odd[k] = (diff_re * cosine - diff_im * sine, diff_re * sine + diff_im * cosine)
    backward_stage(even, store, start, 2 * step)
    backward_stage(odd, store, start + step, 2 * step)


def rows_forward(load_tile, held, rows, outer):
    def body(index, carry):
        at = pl.ds(pl.multiple_of(index * 8, 8), 8)
        spec = forward_stage(lambda tile: load_tile(tile, at), 0, 1, outer)
        held[0, at, :LANES] = spec[0][0]
        held[0, at, LANES:] = spec[outer // 2][0]
        for k in range(1, outer // 2):
            held[k, at, :LANES] = spec[k][0]
            held[k, at, LANES:] = spec[k][1]
        return carry

    lax.fori_loop(0, rows // 8, body, 0)


def rows_backward(store_tile, held, rows, outer):
    def body(index, carry):
        at = pl.ds(pl.multiple_of(index * 8, 8), 8)
        spec = [(held[0, at, :LANES], None)]
        for k in range(1, outer // 2):
            spec.append((held[k, at, :LANES], held[k, at, LANES:]))
        spec.append((held[0, at, LANES:], None))
        backward_stage(spec, lambda tile, value: store_tile(tile, at, value), 0, 1)
        return carry

    lax.fori_loop(0, rows // 8, body, 0)


def pick_kernel(ids, sky, out):
    slots, last = out.shape[0], sky.shape[1] // LANES - 1

    def body(slot, carry):
        at = pl.multiple_of(jnp.minimum(ids[slot], last) * LANES, LANES)
        out[slot] = sky[:, pl.ds(at, LANES)]
        return carry

    lax.fori_loop(0, slots, body, 0)


def sky_forward_kernel(sky, high, low, out, held):
    rows, width = sky.shape
    group = pl.program_id(0)

    @pl.when(group == 0)
    def _():
        def load(tile, at):
            return sky[at, tile * LANES : (tile + 1) * LANES]

        rows_forward(load, held, rows, width // LANES)

    out[0] = multiply(split(held[group]), (high[0], low[0]))


def column_kernel(cols, row_sq, col_sq, f_high, f_low, b_high, b_low, out, held, *, knee_sq):
    length, width = cols.shape
    outer = length // LANES
    group = pl.program_id(0)
    chunks = [(at, min(LANES, width)) for at in range(0, width, LANES)]

    @pl.when(group == 0)
    def _():
        def body(index, carry):
            first = pl.multiple_of(index * 8, 8)
            near, far = pl.ds(first, 8), pl.ds(pl.multiple_of(first + LANES, 8), 8)
            for start, size in chunks:
                lanes = slice(start, start + size)

                def load(tile):
                    return cols[pl.ds(pl.multiple_of(tile * LANES + first, 8), 8), lanes]

                spec = forward_stage(load, 0, 1, outer)
                held[0, near, lanes] = spec[0][0]
                held[0, far, lanes] = spec[outer // 2][0]
                for k in range(1, outer // 2):
                    held[k, near, lanes] = spec[k][0]
                    held[k, far, lanes] = spec[k][1]
            return carry

        lax.fori_loop(0, LANES // 8, body, 0)

    spectrum = multiply((f_high[0], f_low[0]), split(held[group]))
    radial_sq = row_sq[0] + col_sq[...]
    gain = 1.0 + radial_sq * 20.0 + 0.25 * lax.rsqrt(radial_sq + knee_sq)
    held[group] = multiply((b_high[0], b_low[0]), split(spectrum * gain))

    @pl.when(group == pl.num_programs(0) - 1)
    def _():
        def body(index, carry):
            first = pl.multiple_of(index * 8, 8)
            near, far = pl.ds(first, 8), pl.ds(pl.multiple_of(first + LANES, 8), 8)
            for start, size in chunks:
                lanes = slice(start, start + size)
                spec = [(held[0, near, lanes], None)]
                for k in range(1, outer // 2):
                    spec.append((held[k, near, lanes], held[k, far, lanes]))
                spec.append((held[0, far, lanes], None))

                def store(tile, value):
                    out[pl.ds(pl.multiple_of(tile * LANES + first, 8), 8), lanes] = value

                backward_stage(spec, store, 0, 1)
            return carry

        lax.fori_loop(0, LANES // 8, body, 0)


def finish_kernel(ids, spectrum, high, low, delivered, out, held):
    rows, width = out.shape
    group = pl.program_id(0)
    held[group] = multiply(split(spectrum[0]), (high[0], low[0]))

    @pl.when(group == pl.num_programs(0) - 1)
    def _():
        def store(tile, at, value):
            out[at, tile * LANES : (tile + 1) * LANES] = -value

        rows_backward(store, held, rows, width // LANES)

        def body(slot, carry):
            block = ids[slot]

            @pl.when(block < width // LANES)
            def _():
                at = pl.ds(pl.multiple_of(block * LANES, LANES), LANES)
                out[:, at] = out[:, at] + delivered[slot]

            return carry

        lax.fori_loop(0, delivered.shape[0], body, 0)


def data_forward_kernel(
    pointing, slots, arrived, data, beam, white, loading, high, low, spec_out, proj_out, held, listed, tiles
):
    dets, width = data.shape
    outer = width // LANES
    wanted, block_rows = slots.shape[0], arrived.shape[1]
    group = pl.program_id(0)

    @pl.when(group == 0)
    def _():
        def place(entry, carry):
            at = pl.ds(pl.multiple_of(entry * block_rows, 8), block_rows)
            listed[at, :] = arrived[slots[entry]]
            return carry

        lax.fori_loop(0, wanted, place, 0)
        response = split(beam[...])

        def fetch(tile, carry):
            for det in range(dets):
                tiles[tile, det : det + 1, :] = listed[pl.ds(pointing[det, tile], 1), :]
            return carry

        lax.fori_loop(0, outer, fetch, 0)

        for tile in range(outer):
            signal = multiply(split(tiles[tile]), response, (((1,), (1,)), ((), ())))
            tiles[tile] = data[:, tile * LANES : (tile + 1) * LANES] - signal

        rows_forward(lambda tile, at: tiles[tile, at, :], held, dets, outer)

    spec = multiply(split(held[group]), (high[0], low[0]))
    spec_out[0] = spec
    proj_out[0] = multiply(split(loading[...]), split(white[0] * spec), (((0,), (0,)), ((), ())))


def data_backward_kernel(
    pointing, slots, spec, proj, coupling, beam, white, loading, high, low, out, held, tiles, first, second, third, fourth
):
    dets = spec.shape[1]
    modes = proj.shape[1]
    outer = tiles.shape[0]
    wanted, block_rows = slots.shape[0], out.shape[1]
    group = pl.program_id(0)
    coupled = coupling[0, 0] * proj[0, 0:1, :]
    for mode in range(1, modes):
        coupled = coupled + coupling[0, mode] * proj[0, mode : mode + 1, :]
    common = multiply(split(loading[...]), split(coupled))
    filtered = white[0] * (spec[0] - common)
    held[group] = multiply(split(filtered), (high[0], low[0]))

    @pl.when(group == pl.num_programs(0) - 1)
    def _():
        def store(tile, at, value):
            tiles[tile, at, :] = value

        rows_backward(store, held, dets, outer)
        sums = (first, second, third, fourth)
        for total in sums:
            total[...] = jnp.zeros_like(total)
        out[...] = jnp.zeros_like(out)
        response = split(beam[...])
        for tile in range(outer):
            tiles[tile] = multiply(split(tiles[tile]), response)

        def add(tile, carry):
            for det in range(dets):
                total = sums[det % 4]
                at = pl.ds(pointing[det, tile], 1)
                total[at, :] = total[at, :] + tiles[tile, det : det + 1, :]
            return carry

        lax.fori_loop(0, outer, add, 0)

        def place(entry, carry):
            at = pl.ds(pl.multiple_of(entry * block_rows, 8), block_rows)
            out[slots[entry]] = (first[at, :] + second[at, :]) + (third[at, :] + fourth[at, :])
            return carry

        lax.fori_loop(0, wanted, place, 0)


SCALARS = pl.BlockSpec(memory_space=pltpu.SMEM)


def whole(array):
    return pl.BlockSpec(array.shape, lambda g, n=len(array.shape): (0,) * n)


def sliced(array):
    return pl.BlockSpec((1,) + array.shape[1:], lambda g, n=len(array.shape): (g,) + (0,) * (n - 1))


def first_or_rest(array):
    return pl.BlockSpec(
        (1,) + array.shape[1:], lambda g, n=len(array.shape): (jnp.minimum(g, 1),) + (0,) * (n - 1)
    )


PARAMS = pltpu.CompilerParams(vmem_limit_bytes=LIMIT)


def struct(*shape):
    return jax.ShapeDtypeStruct(shape, F32)


def local(
    detector_data,
    sky_map,
    pointing,
    request_owner,
    request_block,
    beam_kernel,
    inv_white,
    mode_loading,
    mode_kernel,
):
    dets, samples = detector_data.shape
    rows_here, map_cols = sky_map.shape
    owners = lax.axis_size("tm")
    devices = lax.axis_size("det") * owners
    tile = beam_kernel.shape[0]
    blocks_here = map_cols // tile
    wanted = request_owner.shape[0]
    capacity = max(2, 2 * wanted // owners)
    slots = owners * capacity
    modes = mode_loading.shape[1]
    bands = inv_white.shape[1]
    per_device = map_cols // devices
    total_rows = rows_here * devices
    wide = 2 * LANES

    row_forward, row_backward = [halves(t) for t in group_tables(map_cols)]
    row_forward = [jnp.asarray(t) for t in row_forward]
    row_backward = [jnp.asarray(t) for t in row_backward]
    if samples == map_cols:
        time_forward, time_backward = row_forward, row_backward
    else:
        time_forward, time_backward = [[jnp.asarray(h) for h in halves(t)] for t in group_tables(samples)]
    col_f, col_b = group_tables(total_rows)
    col_forward = [jnp.asarray(t) for t in halves(col_f.transpose(0, 2, 1))]
    col_backward = [jnp.asarray(t) for t in halves(col_b.transpose(0, 2, 1))]
    groups = map_cols // LANES // 2
    time_groups = samples // LANES // 2
    col_groups = total_rows // LANES // 2

    target = request_owner[:, 0]
    entry = jnp.arange(wanted, dtype=jnp.int32)
    earlier = (target[:, None] == target[None, :]) & (entry[None, :] < entry[:, None])
    slot_index = target * capacity + jnp.sum(earlier.astype(jnp.int32), axis=1)
    named = slot_index[None, :] == jnp.arange(slots, dtype=jnp.int32)[:, None]
    send_ids = blocks_here + jnp.sum(jnp.where(named, request_block[None, :] - blocks_here, 0), axis=1)
    asked_ids = lax.all_to_all(
        send_ids.reshape(owners, capacity), "tm", split_axis=0, concat_axis=0, tiled=True
    ).reshape(-1)

    outgoing = pl.pallas_call(
        pick_kernel,
        in_specs=[SCALARS, pl.BlockSpec(memory_space=pltpu.VMEM)],
        out_specs=pl.BlockSpec(memory_space=pltpu.VMEM),
        out_shape=struct(slots, rows_here, tile),
        compiler_params=PARAMS,
        name="pick_blocks",
    )(asked_ids, sky_map)
    arrived = lax.all_to_all(
        outgoing.reshape(owners, capacity, rows_here, tile), "tm", split_axis=0, concat_axis=0, tiled=True
    ).reshape(slots, rows_here, tile)

    packed = pl.pallas_call(
        sky_forward_kernel,
        grid=(groups,),
        in_specs=[whole(sky_map), sliced(row_forward[0]), sliced(row_forward[1])],
        out_specs=pl.BlockSpec((1, rows_here, wide), lambda g: (g, 0, 0)),
        out_shape=struct(groups, rows_here, wide),
        scratch_shapes=[pltpu.VMEM((groups, rows_here, wide), F32)],
        compiler_params=PARAMS,
        name="sky_forward",
    )(sky_map, *row_forward)
    parts = wide // per_device
    if parts > 1:
        packed = packed.reshape(groups, rows_here, parts, per_device).transpose(0, 2, 1, 3)
        packed = packed.reshape(devices, rows_here, per_device)
    columns = lax.all_to_all(packed, ("det", "tm"), split_axis=0, concat_axis=0, tiled=True)
    columns = columns.reshape(total_rows, per_device)

    freq = group_frequencies(samples)[:2]
    band = np.minimum(np.minimum(freq, samples - freq) // BAND_WIDTH, bands - 1)
    onehot = jnp.asarray((np.arange(bands)[:, None, None] == band[None]).astype(np.float32))
    precise = lax.Precision.HIGHEST
    white = jnp.einsum("jb,bgf->gjf", inv_white, onehot, precision=precise)
    coupling = jnp.einsum("bmn,bgf->gnmf", mode_kernel, onehot, precision=precise)
    spec, proj = pl.pallas_call(
        data_forward_kernel,
        grid=(time_groups,),
        in_specs=[
            SCALARS,
            SCALARS,
            whole(arrived),
            whole(detector_data),
            whole(beam_kernel),
            first_or_rest(white),
            whole(mode_loading),
            sliced(time_forward[0]),
            sliced(time_forward[1]),
        ],
        out_specs=[
            pl.BlockSpec((1, dets, wide), lambda g: (g, 0, 0)),
            pl.BlockSpec((1, modes, wide), lambda g: (g, 0, 0)),
        ],
        out_shape=[struct(time_groups, dets, wide), struct(time_groups, modes, wide)],
        scratch_shapes=[
            pltpu.VMEM((time_groups, dets, wide), F32),
            pltpu.VMEM((wanted * rows_here, tile), F32),
            pltpu.VMEM((samples // tile, dets, tile), F32),
        ],
        compiler_params=PARAMS,
        name="data_forward",
    )(pointing, slot_index, arrived, detector_data, beam_kernel, white, mode_loading, *time_forward)
    proj = lax.psum(proj, "det")

    returned = pl.pallas_call(
        data_backward_kernel,
        grid=(time_groups,),
        in_specs=[
            SCALARS,
            SCALARS,
            sliced(spec),
            sliced(proj),
            first_or_rest(coupling),
            whole(beam_kernel),
            first_or_rest(white),
            whole(mode_loading),
            sliced(time_backward[0]),
            sliced(time_backward[1]),
        ],
        out_specs=pl.BlockSpec((slots, rows_here, tile), lambda g: (0, 0, 0)),
        out_shape=struct(slots, rows_here, tile),
        scratch_shapes=[
            pltpu.VMEM((time_groups, dets, wide), F32),
            pltpu.VMEM((samples // tile, dets, tile), F32),
        ]
        + [pltpu.VMEM((wanted * rows_here, tile), F32)] * 4,
        compiler_params=PARAMS,
        name="data_backward",
    )(pointing, slot_index, spec, proj, coupling, beam_kernel, white, mode_loading, *time_backward)
    delivered = lax.all_to_all(
        returned.reshape(owners, capacity, rows_here, tile), "tm", split_axis=0, concat_axis=0, tiled=True
    ).reshape(slots, rows_here, tile)

    rank = lax.axis_index("det") * owners + lax.axis_index("tm")
    col_freq = group_frequencies(map_cols).reshape(-1)
    col_sq = (np.minimum(col_freq, map_cols - col_freq) / map_cols) ** 2
    col_sq = lax.dynamic_slice_in_dim(
        jnp.asarray(col_sq.astype(np.float32).reshape(devices, per_device)), rank, 1, 0
    )
    row_freq = group_frequencies(total_rows)
    row_sq = ((np.minimum(row_freq, total_rows - row_freq) / total_rows) ** 2).astype(np.float32)
    row_sq = jnp.asarray(row_sq[:, :, None])
    knee_sq = 1.0 / (2.0 * math.pi * total_rows / 64.0) ** 2
    backed = pl.pallas_call(
        functools.partial(column_kernel, knee_sq=knee_sq),
        grid=(col_groups,),
        in_specs=[whole(columns), sliced(row_sq), whole(col_sq)]
        + [sliced(t) for t in col_forward + col_backward],
        out_specs=pl.BlockSpec((total_rows, per_device), lambda g: (0, 0)),
        out_shape=struct(total_rows, per_device),
        scratch_shapes=[pltpu.VMEM((col_groups, wide, per_device), F32)],
        compiler_params=PARAMS,
        name="sky_columns",
    )(columns, row_sq, col_sq, *col_forward, *col_backward)
    spectrum = lax.all_to_all(
        backed.reshape(devices, rows_here, per_device),
        ("det", "tm"),
        split_axis=0,
        concat_axis=0,
        tiled=True,
    )
    if parts > 1:
        spectrum = spectrum.reshape(groups, parts, rows_here, per_device).transpose(0, 2, 1, 3)
        spectrum = spectrum.reshape(groups, rows_here, wide)

    return pl.pallas_call(
        finish_kernel,
        grid=(groups,),
        in_specs=[
            SCALARS,
            sliced(spectrum),
            sliced(row_backward[0]),
            sliced(row_backward[1]),
            whole(delivered),
        ],
        out_specs=pl.BlockSpec((rows_here, map_cols), lambda g: (0, 0)),
        out_shape=struct(rows_here, map_cols),
        scratch_shapes=[pltpu.VMEM((groups, rows_here, wide), F32)],
        compiler_params=PARAMS,
        name="sky_finish",
    )(asked_ids, spectrum, *row_backward, delivered)


def solution(mesh):
    return jax.shard_map(
        local,
        mesh=mesh,
        in_specs=(
            P("det", "tm"),
            P(("det", "tm"), None),
            P("det", "tm"),
            P(("det", "tm"), None),
            P(("det", "tm")),
            P(),
            P("det", None),
            P("det", None),
            P(),
        ),
        out_specs=P(("det", "tm"), None),
        check_vma=False,
    )
```

```python
import functools
import math

import jax
import jax.numpy as jnp
import ml_dtypes
import numpy as np
from jax import lax
from jax.experimental import pallas as pl
from jax.experimental.pallas import tpu as pltpu
from jax.sharding import PartitionSpec as P

BAND_WIDTH = 128
LANES = 128
BATCH = 4
LIMIT = 50 * 1024 * 1024
F32 = jnp.float32
BF16 = jnp.bfloat16


def group_frequencies(length):
    half = LANES // 2
    outer = length // LANES
    steps = np.arange(LANES)
    freq = np.zeros((outer // 2, 2 * LANES), np.int64)
    for group in range(1, outer // 2):
        freq[group] = np.concatenate([group + outer * steps] * 2)
    low = outer * np.concatenate([np.arange(half + 1), np.arange(1, half)])
    middle = outer // 2 + outer * np.concatenate([np.arange(half)] * 2)
    freq[0] = np.concatenate([low, middle])
    return freq


def group_tables(length):
    half = LANES // 2
    freq = group_frequencies(length)
    groups = freq.shape[0]
    steps = np.arange(LANES)
    forward = np.zeros((groups, 2 * LANES, 2 * LANES))
    weight = np.ones((groups, 2 * LANES))
    angle = 2.0 * math.pi / length
    for group in range(groups):
        turn = (steps[:, None] * freq[group][None, :] % length) * angle
        cosine, sine = np.cos(turn), np.sin(turn)
        if group > 0:
            forward[group, :LANES, :LANES] = cosine[:, :LANES]
            forward[group, LANES:, :LANES] = sine[:, :LANES]
            forward[group, :LANES, LANES:] = -sine[:, LANES:]
            forward[group, LANES:, LANES:] = cosine[:, LANES:]
        else:
            forward[0, :LANES, : half + 1] = cosine[:, : half + 1]
            forward[0, :LANES, half + 1 : LANES] = -sine[:, half + 1 : LANES]
            forward[0, LANES:, LANES : LANES + half] = cosine[:, LANES : LANES + half]
            forward[0, LANES:, LANES + half :] = -sine[:, LANES + half :]
            weight[0, :] = 2.0
            weight[0, 0] = 1.0
            weight[0, half] = 1.0
    backward = (forward * weight[:, None, :] / length).transpose(0, 2, 1)
    return forward, backward


def halves(table):
    high = table.astype(np.float32).astype(ml_dtypes.bfloat16)
    low = (table - high.astype(np.float64)).astype(ml_dtypes.bfloat16)
    return high, low


def split(value):
    high = value.astype(BF16)
    return high, (value - high.astype(F32)).astype(BF16)


def multiply(left, right, dims=(((1,), (0,)), ((), ()))):
    dot = functools.partial(lax.dot_general, dimension_numbers=dims, preferred_element_type=F32)
    return dot(left[0], right[0]) + (dot(left[1], right[0]) + dot(left[0], right[1]))


def forward_stage(load, start, step, count):
    if count == 2:
        first, second = load(start), load(start + step)
        return [(first + second, None), (first - second, None)]
    even = forward_stage(load, start, 2 * step, count // 2)
    odd = forward_stage(load, start + step, 2 * step, count // 2)
    out = [None] * (count // 2 + 1)
    out[0] = (even[0][0] + odd[0][0], None)
    out[count // 2] = (even[0][0] - odd[0][0], None)
    out[count // 4] = (even[count // 4][0], -odd[count // 4][0])
    for k in range(1, count // 4):
        cosine, sine = math.cos(2 * math.pi * k / count), math.sin(2 * math.pi * k / count)
        odd_re, odd_im = odd[k]
        turn_re = cosine * odd_re + sine * odd_im
        turn_im = cosine * odd_im - sine * odd_re
        out[k] = (even[k][0] + turn_re, even[k][1] + turn_im)
        out[count // 2 - k] = (even[k][0] - turn_re, turn_im - even[k][1])
    return out


def backward_stage(spec, store, start, step):
    count = 2 * (len(spec) - 1)
    if count == 2:
        store(start, spec[0][0] + spec[1][0])
        store(start + step, spec[0][0] - spec[1][0])
        return
    even, odd = [None] * (count // 4 + 1), [None] * (count // 4 + 1)
    even[0] = (spec[0][0] + spec[count // 2][0], None)
    odd[0] = (spec[0][0] - spec[count // 2][0], None)
    middle = spec[count // 4]
    even[count // 4] = (2.0 * middle[0], None)
    odd[count // 4] = (-2.0 * middle[1], None)
    for k in range(1, count // 4):
        cosine, sine = math.cos(2 * math.pi * k / count), math.sin(2 * math.pi * k / count)
        (a_re, a_im), (b_re, b_im) = spec[k], spec[count // 2 - k]
        even[k] = (a_re + b_re, a_im - b_im)
        diff_re, diff_im = a_re - b_re, a_im + b_im
        odd[k] = (diff_re * cosine - diff_im * sine, diff_re * sine + diff_im * cosine)
    backward_stage(even, store, start, 2 * step)
    backward_stage(odd, store, start + step, 2 * step)


def rows_forward(load_tile, held, rows, outer):
    def body(index, carry):
        at = pl.ds(pl.multiple_of(index * 8, 8), 8)
        spec = forward_stage(lambda tile: load_tile(tile, at), 0, 1, outer)
        held[0, at, :LANES] = spec[0][0]
        held[0, at, LANES:] = spec[outer // 2][0]
        for k in range(1, outer // 2):
            held[k, at, :LANES] = spec[k][0]
            held[k, at, LANES:] = spec[k][1]
        return carry

    lax.fori_loop(0, rows // 8, body, 0)


def rows_backward(store_tile, held, rows, outer):
    def body(index, carry):
        at = pl.ds(pl.multiple_of(index * 8, 8), 8)
        spec = [(held[0, at, :LANES], None)]
        for k in range(1, outer // 2):
            spec.append((held[k, at, :LANES], held[k, at, LANES:]))
        spec.append((held[0, at, LANES:], None))
        backward_stage(spec, lambda tile, value: store_tile(tile, at, value), 0, 1)
        return carry

    lax.fori_loop(0, rows // 8, body, 0)


def pick_kernel(ids, sky, out):
    slots, last = out.shape[0], sky.shape[1] // LANES - 1

    def body(slot, carry):
        at = pl.multiple_of(jnp.minimum(ids[slot], last) * LANES, LANES)
        out[slot] = sky[:, pl.ds(at, LANES)]
        return carry

    lax.fori_loop(0, slots, body, 0)


def sky_forward_kernel(sky, high, low, out, held):
    rows, width = sky.shape
    step = pl.program_id(0)

    @pl.when(step == 0)
    def _():
        def load(tile, at):
            return sky[at, tile * LANES : (tile + 1) * LANES]

        rows_forward(load, held, rows, width // LANES)

    for i in range(BATCH):
        out[i] = multiply(split(held[step * BATCH + i]), (high[i], low[i]))


def column_kernel(cols, row_sq, col_sq, f_high, f_low, b_high, b_low, out, held, *, knee_sq):
    length, width = cols.shape
    outer = length // LANES
    step = pl.program_id(0)
    chunks = [(at, min(LANES, width)) for at in range(0, width, LANES)]

    @pl.when(step == 0)
    def _():
        def body(index, carry):
            first = pl.multiple_of(index * 8, 8)
            near, far = pl.ds(first, 8), pl.ds(pl.multiple_of(first + LANES, 8), 8)
            for start, size in chunks:
                lanes = slice(start, start + size)

                def load(tile):
                    return cols[pl.ds(pl.multiple_of(tile * LANES + first, 8), 8), lanes]

                spec = forward_stage(load, 0, 1, outer)
                held[0, near, lanes] = spec[0][0]
                held[0, far, lanes] = spec[outer // 2][0]
                for k in range(1, outer // 2):
                    held[k, near, lanes] = spec[k][0]
                    held[k, far, lanes] = spec[k][1]
            return carry

        lax.fori_loop(0, LANES // 8, body, 0)

    for i in range(BATCH):
        group = step * BATCH + i
        spectrum = multiply((f_high[i], f_low[i]), split(held[group]))
        radial_sq = row_sq[i] + col_sq[...]
        gain = 1.0 + radial_sq * 20.0 + 0.25 * lax.rsqrt(radial_sq + knee_sq)
        held[group] = multiply((b_high[i], b_low[i]), split(spectrum * gain))

    @pl.when(step == pl.num_programs(0) - 1)
    def _():
        def body(index, carry):
            first = pl.multiple_of(index * 8, 8)
            near, far = pl.ds(first, 8), pl.ds(pl.multiple_of(first + LANES, 8), 8)
            for start, size in chunks:
                lanes = slice(start, start + size)
                spec = [(held[0, near, lanes], None)]
                for k in range(1, outer // 2):
                    spec.append((held[k, near, lanes], held[k, far, lanes]))
                spec.append((held[0, far, lanes], None))

                def store(tile, value):
                    out[pl.ds(pl.multiple_of(tile * LANES + first, 8), 8), lanes] = value

                backward_stage(spec, store, 0, 1)
            return carry

        lax.fori_loop(0, LANES // 8, body, 0)


def sky_backward_kernel(spectrum, high, low, out, held):
    rows, width = out.shape
    step = pl.program_id(0)
    for i in range(BATCH):
        held[step * BATCH + i] = multiply(split(spectrum[i]), (high[i], low[i]))

    @pl.when(step == pl.num_programs(0) - 1)
    def _():
        def store(tile, at, value):
            out[at, tile * LANES : (tile + 1) * LANES] = -value

        rows_backward(store, held, rows, width // LANES)


def finish_kernel(ids, base, delivered, out):
    out[...] = base[...]

    def body(slot, carry):
        block = ids[slot]

        @pl.when(block < out.shape[1] // LANES)
        def _():
            at = pl.ds(pl.multiple_of(block * LANES, LANES), LANES)
            out[:, at] = out[:, at] + delivered[slot]

        return carry

    lax.fori_loop(0, delivered.shape[0], body, 0)


def data_forward_kernel(
    pointing, slots, arrived, data, beam, white, loading, high, low, spec_out, proj_out, held, listed, tiles
):
    dets, width = data.shape
    outer = width // LANES
    wanted, block_rows = slots.shape[0], arrived.shape[1]
    step = pl.program_id(0)

    @pl.when(step == 0)
    def _():
        def place(entry, carry):
            at = pl.ds(pl.multiple_of(entry * block_rows, 8), block_rows)
            listed[at, :] = arrived[slots[entry]]
            return carry

        lax.fori_loop(0, wanted, place, 0)
        response = split(beam[...])

        def fetch(tile, carry):
            for det in range(dets):
                tiles[tile, det : det + 1, :] = listed[pl.ds(pointing[det, tile], 1), :]
            return carry

        lax.fori_loop(0, outer, fetch, 0)

        for tile in range(outer):
            signal = multiply(split(tiles[tile]), response, (((1,), (1,)), ((), ())))
            tiles[tile] = data[:, tile * LANES : (tile + 1) * LANES] - signal

        rows_forward(lambda tile, at: tiles[tile, at, :], held, dets, outer)

    for i in range(BATCH):
        group = step * BATCH + i
        spec = multiply(split(held[group]), (high[i], low[i]))
        spec_out[i] = spec
        weighted = white[jnp.minimum(group, 1)] * spec
        proj_out[i] = multiply(split(loading[...]), split(weighted), (((0,), (0,)), ((), ())))


def data_backward_kernel(
    pointing, slots, spec, proj, coupling, beam, white, loading, high, low, out, held, tiles, first, second, third, fourth
):
    dets = spec.shape[1]
    modes = proj.shape[1]
    outer = tiles.shape[0]
    wanted, block_rows = slots.shape[0], out.shape[1]
    step = pl.program_id(0)
    for i in range(BATCH):
        group = step * BATCH + i
        kind = jnp.minimum(group, 1)
        coupled = coupling[kind, 0] * proj[i, 0:1, :]
        for mode in range(1, modes):
            coupled = coupled + coupling[kind, mode] * proj[i, mode : mode + 1, :]
        common = multiply(split(loading[...]), split(coupled))
        filtered = white[kind] * (spec[i] - common)
        held[group] = multiply(split(filtered), (high[i], low[i]))

    @pl.when(step == pl.num_programs(0) - 1)
    def _():
        def store(tile, at, value):
            tiles[tile, at, :] = value

        rows_backward(store, held, dets, outer)
        sums = (first, second, third, fourth)
        for total in sums:
            total[...] = jnp.zeros_like(total)
        out[...] = jnp.zeros_like(out)
        response = split(beam[...])
        for tile in range(outer):
            tiles[tile] = multiply(split(tiles[tile]), response)

        def add(tile, carry):
            for det in range(dets):
                total = sums[det % 4]
                at = pl.ds(pointing[det, tile], 1)
                total[at, :] = total[at, :] + tiles[tile, det : det + 1, :]
            return carry

        lax.fori_loop(0, outer, add, 0)

        def place(entry, carry):
            at = pl.ds(pl.multiple_of(entry * block_rows, 8), block_rows)
            out[slots[entry]] = (first[at, :] + second[at, :]) + (third[at, :] + fourth[at, :])
            return carry

        lax.fori_loop(0, wanted, place, 0)


SCALARS = pl.BlockSpec(memory_space=pltpu.SMEM)


def whole(array):
    return pl.BlockSpec(array.shape, lambda g, n=len(array.shape): (0,) * n)


def sliced(array):
    return pl.BlockSpec((BATCH,) + array.shape[1:], lambda g, n=len(array.shape): (g,) + (0,) * (n - 1))


PARAMS = pltpu.CompilerParams(vmem_limit_bytes=LIMIT)


def struct(*shape):
    return jax.ShapeDtypeStruct(shape, F32)


def local(
    detector_data,
    sky_map,
    pointing,
    request_owner,
    request_block,
    beam_kernel,
    inv_white,
    mode_loading,
    mode_kernel,
):
    dets, samples = detector_data.shape
    rows_here, map_cols = sky_map.shape
    owners = lax.axis_size("tm")
    devices = lax.axis_size("det") * owners
    tile = beam_kernel.shape[0]
    blocks_here = map_cols // tile
    wanted = request_owner.shape[0]
    capacity = max(2, 2 * wanted // owners)
    slots = owners * capacity
    modes = mode_loading.shape[1]
    bands = inv_white.shape[1]
    per_device = map_cols // devices
    total_rows = rows_here * devices
    wide = 2 * LANES

    row_forward, row_backward = [halves(t) for t in group_tables(map_cols)]
    row_forward = [jnp.asarray(t) for t in row_forward]
    row_backward = [jnp.asarray(t) for t in row_backward]
    if samples == map_cols:
        time_forward, time_backward = row_forward, row_backward
    else:
        time_forward, time_backward = [[jnp.asarray(h) for h in halves(t)] for t in group_tables(samples)]
    col_f, col_b = group_tables(total_rows)
    col_forward = [jnp.asarray(t) for t in halves(col_f.transpose(0, 2, 1))]
    col_backward = [jnp.asarray(t) for t in halves(col_b.transpose(0, 2, 1))]
    groups = map_cols // LANES // 2
    time_groups = samples // LANES // 2
    col_groups = total_rows // LANES // 2

    target = request_owner[:, 0]
    entry = jnp.arange(wanted, dtype=jnp.int32)
    earlier = (target[:, None] == target[None, :]) & (entry[None, :] < entry[:, None])
    slot_index = target * capacity + jnp.sum(earlier.astype(jnp.int32), axis=1)
    named = slot_index[None, :] == jnp.arange(slots, dtype=jnp.int32)[:, None]
    send_ids = blocks_here + jnp.sum(jnp.where(named, request_block[None, :] - blocks_here, 0), axis=1)
    all_ids = lax.all_gather(send_ids, "tm", axis=0).reshape(owners, owners, capacity)
    asked_ids = lax.dynamic_index_in_dim(all_ids, lax.axis_index("tm"), 1, False).reshape(-1)

    outgoing = pl.pallas_call(
        pick_kernel,
        in_specs=[SCALARS, pl.BlockSpec(memory_space=pltpu.VMEM)],
        out_specs=pl.BlockSpec(memory_space=pltpu.VMEM),
        out_shape=struct(slots, rows_here, tile),
        compiler_params=PARAMS,
        name="pick_blocks",
    )(asked_ids, sky_map)
    packed = pl.pallas_call(
        sky_forward_kernel,
        grid=(groups // BATCH,),
        in_specs=[whole(sky_map), sliced(row_forward[0]), sliced(row_forward[1])],
        out_specs=pl.BlockSpec((BATCH, rows_here, wide), lambda g: (g, 0, 0)),
        out_shape=struct(groups, rows_here, wide),
        scratch_shapes=[pltpu.VMEM((groups, rows_here, wide), F32)],
        compiler_params=PARAMS,
        name="sky_forward",
    )(sky_map, *row_forward)
    parts = wide // per_device
    if parts > 1:
        packed = packed.reshape(groups, rows_here, parts, per_device).transpose(0, 2, 1, 3)
        packed = packed.reshape(devices, rows_here, per_device)
    columns = lax.all_to_all(packed, ("det", "tm"), split_axis=0, concat_axis=0, tiled=True)
    columns, outgoing = lax.optimization_barrier((columns, outgoing))
    columns = columns.reshape(total_rows, per_device)
    arrived = lax.all_to_all(
        outgoing.reshape(owners, capacity, rows_here, tile), "tm", split_axis=0, concat_axis=0, tiled=True
    ).reshape(slots, rows_here, tile)

    rank = lax.axis_index("det") * owners + lax.axis_index("tm")
    col_freq = group_frequencies(map_cols).reshape(-1)
    col_sq = (np.minimum(col_freq, map_cols - col_freq) / map_cols) ** 2
    col_sq = lax.dynamic_slice_in_dim(
        jnp.asarray(col_sq.astype(np.float32).reshape(devices, per_device)), rank, 1, 0
    )
    row_freq = group_frequencies(total_rows)
    row_sq = ((np.minimum(row_freq, total_rows - row_freq) / total_rows) ** 2).astype(np.float32)
    row_sq = jnp.asarray(row_sq[:, :, None])
    knee_sq = 1.0 / (2.0 * math.pi * total_rows / 64.0) ** 2
    backed = pl.pallas_call(
        functools.partial(column_kernel, knee_sq=knee_sq),
        grid=(col_groups // BATCH,),
        in_specs=[whole(columns), sliced(row_sq), whole(col_sq)]
        + [sliced(t) for t in col_forward + col_backward],
        out_specs=pl.BlockSpec((total_rows, per_device), lambda g: (0, 0)),
        out_shape=struct(total_rows, per_device),
        scratch_shapes=[pltpu.VMEM((col_groups, wide, per_device), F32)],
        compiler_params=PARAMS,
        name="sky_columns",
    )(columns, row_sq, col_sq, *col_forward, *col_backward)
    backed, arrived = lax.optimization_barrier((backed, arrived))
    spectrum = lax.all_to_all(
        backed.reshape(devices, rows_here, per_device),
        ("det", "tm"),
        split_axis=0,
        concat_axis=0,
        tiled=True,
    )
    if parts > 1:
        spectrum = spectrum.reshape(groups, parts, rows_here, per_device).transpose(0, 2, 1, 3)
        spectrum = spectrum.reshape(groups, rows_here, wide)

    freq = group_frequencies(samples)[:2]
    band = np.minimum(np.minimum(freq, samples - freq) // BAND_WIDTH, bands - 1)
    onehot = jnp.asarray((np.arange(bands)[:, None, None] == band[None]).astype(np.float32))
    precise = lax.Precision.HIGHEST
    white = jnp.einsum("jb,bgf->gjf", inv_white, onehot, precision=precise)
    coupling = jnp.einsum("bmn,bgf->gnmf", mode_kernel, onehot, precision=precise)
    spec, proj = pl.pallas_call(
        data_forward_kernel,
        grid=(time_groups // BATCH,),
        in_specs=[
            SCALARS,
            SCALARS,
            whole(arrived),
            whole(detector_data),
            whole(beam_kernel),
            whole(white),
            whole(mode_loading),
            sliced(time_forward[0]),
            sliced(time_forward[1]),
        ],
        out_specs=[
            pl.BlockSpec((BATCH, dets, wide), lambda g: (g, 0, 0)),
            pl.BlockSpec((BATCH, modes, wide), lambda g: (g, 0, 0)),
        ],
        out_shape=[struct(time_groups, dets, wide), struct(time_groups, modes, wide)],
        scratch_shapes=[
            pltpu.VMEM((time_groups, dets, wide), F32),
            pltpu.VMEM((wanted * rows_here, tile), F32),
            pltpu.VMEM((samples // tile, dets, tile), F32),
        ],
        compiler_params=PARAMS,
        name="data_forward",
    )(pointing, slot_index, arrived, detector_data, beam_kernel, white, mode_loading, *time_forward)
    proj = lax.psum(proj, "det")

    returned = pl.pallas_call(
        data_backward_kernel,
        grid=(time_groups // BATCH,),
        in_specs=[
            SCALARS,
            SCALARS,
            sliced(spec),
            sliced(proj),
            whole(coupling),
            whole(beam_kernel),
            whole(white),
            whole(mode_loading),
            sliced(time_backward[0]),
            sliced(time_backward[1]),
        ],
        out_specs=pl.BlockSpec((slots, rows_here, tile), lambda g: (0, 0, 0)),
        out_shape=struct(slots, rows_here, tile),
        scratch_shapes=[
            pltpu.VMEM((time_groups, dets, wide), F32),
            pltpu.VMEM((samples // tile, dets, tile), F32),
        ]
        + [pltpu.VMEM((wanted * rows_here, tile), F32)] * 4,
        compiler_params=PARAMS,
        name="data_backward",
    )(pointing, slot_index, spec, proj, coupling, beam_kernel, white, mode_loading, *time_backward)
    returned, spectrum = lax.optimization_barrier((returned, spectrum))
    delivered = lax.all_to_all(
        returned.reshape(owners, capacity, rows_here, tile), "tm", split_axis=0, concat_axis=0, tiled=True
    ).reshape(slots, rows_here, tile)

    base = pl.pallas_call(
        sky_backward_kernel,
        grid=(groups // BATCH,),
        in_specs=[sliced(spectrum), sliced(row_backward[0]), sliced(row_backward[1])],
        out_specs=pl.BlockSpec((rows_here, map_cols), lambda g: (0, 0)),
        out_shape=struct(rows_here, map_cols),
        scratch_shapes=[pltpu.VMEM((groups, rows_here, wide), F32)],
        compiler_params=PARAMS,
        name="sky_backward",
    )(spectrum, *row_backward)

    chunk = rows_here // 4
    return pl.pallas_call(
        finish_kernel,
        grid=(4,),
        in_specs=[
            SCALARS,
            pl.BlockSpec((chunk, map_cols), lambda g: (g, 0)),
            pl.BlockSpec((slots, chunk, tile), lambda g: (0, g, 0)),
        ],
        out_specs=pl.BlockSpec((chunk, map_cols), lambda g: (g, 0)),
        out_shape=struct(rows_here, map_cols),
        compiler_params=PARAMS,
        name="sky_finish",
    )(asked_ids, base, delivered)


def solution(mesh):
    return jax.shard_map(
        local,
        mesh=mesh,
        in_specs=(
            P("det", "tm"),
            P(("det", "tm"), None),
            P("det", "tm"),
            P(("det", "tm"), None),
            P(("det", "tm")),
            P(),
            P("det", None),
            P("det", None),
            P(),
        ),
        out_specs=P(("det", "tm"), None),
        check_vma=False,
    )
```

```python
import functools
import math

import jax
import jax.numpy as jnp
import ml_dtypes
import numpy as np
from jax import lax
from jax.experimental import pallas as pl
from jax.experimental.pallas import tpu as pltpu
from jax.sharding import PartitionSpec as P

BAND_WIDTH = 128
LANES = 128
BATCH = 4
LIMIT = 50 * 1024 * 1024
F32 = jnp.float32
BF16 = jnp.bfloat16


def group_frequencies(length):
    half = LANES // 2
    outer = length // LANES
    steps = np.arange(LANES)
    freq = np.zeros((outer // 2, 2 * LANES), np.int64)
    for group in range(1, outer // 2):
        freq[group] = np.concatenate([group + outer * steps] * 2)
    low = outer * np.concatenate([np.arange(half + 1), np.arange(1, half)])
    middle = outer // 2 + outer * np.concatenate([np.arange(half)] * 2)
    freq[0] = np.concatenate([low, middle])
    return freq


def group_tables(length):
    half = LANES // 2
    freq = group_frequencies(length)
    groups = freq.shape[0]
    steps = np.arange(LANES)
    forward = np.zeros((groups, 2 * LANES, 2 * LANES))
    weight = np.ones((groups, 2 * LANES))
    angle = 2.0 * math.pi / length
    for group in range(groups):
        turn = (steps[:, None] * freq[group][None, :] % length) * angle
        cosine, sine = np.cos(turn), np.sin(turn)
        if group > 0:
            forward[group, :LANES, :LANES] = cosine[:, :LANES]
            forward[group, LANES:, :LANES] = sine[:, :LANES]
            forward[group, :LANES, LANES:] = -sine[:, LANES:]
            forward[group, LANES:, LANES:] = cosine[:, LANES:]
        else:
            forward[0, :LANES, : half + 1] = cosine[:, : half + 1]
            forward[0, :LANES, half + 1 : LANES] = -sine[:, half + 1 : LANES]
            forward[0, LANES:, LANES : LANES + half] = cosine[:, LANES : LANES + half]
            forward[0, LANES:, LANES + half :] = -sine[:, LANES + half :]
            weight[0, :] = 2.0
            weight[0, 0] = 1.0
            weight[0, half] = 1.0
    backward = (forward * weight[:, None, :] / length).transpose(0, 2, 1)
    return forward, backward


def halves(table):
    high = table.astype(np.float32).astype(ml_dtypes.bfloat16)
    low = (table - high.astype(np.float64)).astype(ml_dtypes.bfloat16)
    return high, low


def split(value):
    high = value.astype(BF16)
    return high, (value - high.astype(F32)).astype(BF16)


def multiply(left, right, dims=(((1,), (0,)), ((), ()))):
    dot = functools.partial(lax.dot_general, dimension_numbers=dims, preferred_element_type=F32)
    return dot(left[0], right[0]) + (dot(left[1], right[0]) + dot(left[0], right[1]))


def forward_stage(load, start, step, count):
    if count == 2:
        first, second = load(start), load(start + step)
        return [(first + second, None), (first - second, None)]
    even = forward_stage(load, start, 2 * step, count // 2)
    odd = forward_stage(load, start + step, 2 * step, count // 2)
    out = [None] * (count // 2 + 1)
    out[0] = (even[0][0] + odd[0][0], None)
    out[count // 2] = (even[0][0] - odd[0][0], None)
    out[count // 4] = (even[count // 4][0], -odd[count // 4][0])
    for k in range(1, count // 4):
        cosine, sine = math.cos(2 * math.pi * k / count), math.sin(2 * math.pi * k / count)
        odd_re, odd_im = odd[k]
        turn_re = cosine * odd_re + sine * odd_im
        turn_im = cosine * odd_im - sine * odd_re
        out[k] = (even[k][0] + turn_re, even[k][1] + turn_im)
        out[count // 2 - k] = (even[k][0] - turn_re, turn_im - even[k][1])
    return out


def backward_stage(spec, store, start, step):
    count = 2 * (len(spec) - 1)
    if count == 2:
        store(start, spec[0][0] + spec[1][0])
        store(start + step, spec[0][0] - spec[1][0])
        return
    even, odd = [None] * (count // 4 + 1), [None] * (count // 4 + 1)
    even[0] = (spec[0][0] + spec[count // 2][0], None)
    odd[0] = (spec[0][0] - spec[count // 2][0], None)
    middle = spec[count // 4]
    even[count // 4] = (2.0 * middle[0], None)
    odd[count // 4] = (-2.0 * middle[1], None)
    for k in range(1, count // 4):
        cosine, sine = math.cos(2 * math.pi * k / count), math.sin(2 * math.pi * k / count)
        (a_re, a_im), (b_re, b_im) = spec[k], spec[count // 2 - k]
        even[k] = (a_re + b_re, a_im - b_im)
        diff_re, diff_im = a_re - b_re, a_im + b_im
        odd[k] = (diff_re * cosine - diff_im * sine, diff_re * sine + diff_im * cosine)
    backward_stage(even, store, start, 2 * step)
    backward_stage(odd, store, start + step, 2 * step)


def rows_forward(load_tile, held, rows, outer):
    def body(index, carry):
        at = pl.ds(pl.multiple_of(index * 8, 8), 8)
        spec = forward_stage(lambda tile: load_tile(tile, at), 0, 1, outer)
        held[0, at, :LANES] = spec[0][0]
        held[0, at, LANES:] = spec[outer // 2][0]
        for k in range(1, outer // 2):
            held[k, at, :LANES] = spec[k][0]
            held[k, at, LANES:] = spec[k][1]
        return carry

    lax.fori_loop(0, rows // 8, body, 0)


def rows_backward(store_tile, held, rows, outer):
    def body(index, carry):
        at = pl.ds(pl.multiple_of(index * 8, 8), 8)
        spec = [(held[0, at, :LANES], None)]
        for k in range(1, outer // 2):
            spec.append((held[k, at, :LANES], held[k, at, LANES:]))
        spec.append((held[0, at, LANES:], None))
        backward_stage(spec, lambda tile, value: store_tile(tile, at, value), 0, 1)
        return carry

    lax.fori_loop(0, rows // 8, body, 0)


def pick_kernel(ids, sky, out):
    slots, last = out.shape[0], sky.shape[1] // LANES - 1

    def body(slot, carry):
        at = pl.multiple_of(jnp.minimum(ids[slot], last) * LANES, LANES)
        out[slot] = sky[:, pl.ds(at, LANES)]
        return carry

    lax.fori_loop(0, slots, body, 0)


def sky_forward_kernel(sky, high, low, out, held):
    rows, width = sky.shape
    step = pl.program_id(0)

    @pl.when(step == 0)
    def _():
        def load(tile, at):
            return sky[at, tile * LANES : (tile + 1) * LANES]

        rows_forward(load, held, rows, width // LANES)

    for i in range(BATCH):
        out[i] = multiply(split(held[step * BATCH + i]), (high[i], low[i]))


def column_kernel(cols, row_sq, col_sq, f_high, f_low, b_high, b_low, out, held, *, knee_sq):
    length, width = cols.shape
    outer = length // LANES
    step = pl.program_id(0)
    chunks = [(at, min(LANES, width)) for at in range(0, width, LANES)]

    @pl.when(step == 0)
    def _():
        def body(index, carry):
            first = pl.multiple_of(index * 8, 8)
            near, far = pl.ds(first, 8), pl.ds(pl.multiple_of(first + LANES, 8), 8)
            for start, size in chunks:
                lanes = slice(start, start + size)

                def load(tile):
                    return cols[pl.ds(pl.multiple_of(tile * LANES + first, 8), 8), lanes]

                spec = forward_stage(load, 0, 1, outer)
                held[0, near, lanes] = spec[0][0]
                held[0, far, lanes] = spec[outer // 2][0]
                for k in range(1, outer // 2):
                    held[k, near, lanes] = spec[k][0]
                    held[k, far, lanes] = spec[k][1]
            return carry

        lax.fori_loop(0, LANES // 8, body, 0)

    for i in range(BATCH):
        group = step * BATCH + i
        spectrum = multiply((f_high[i], f_low[i]), split(held[group]))
        radial_sq = row_sq[i] + col_sq[...]
        gain = 1.0 + radial_sq * 20.0 + 0.25 * lax.rsqrt(radial_sq + knee_sq)
        held[group] = multiply((b_high[i], b_low[i]), split(spectrum * gain))

    @pl.when(step == pl.num_programs(0) - 1)
    def _():
        def body(index, carry):
            first = pl.multiple_of(index * 8, 8)
            near, far = pl.ds(first, 8), pl.ds(pl.multiple_of(first + LANES, 8), 8)
            for start, size in chunks:
                lanes = slice(start, start + size)
                spec = [(held[0, near, lanes], None)]
                for k in range(1, outer // 2):
                    spec.append((held[k, near, lanes], held[k, far, lanes]))
                spec.append((held[0, far, lanes], None))

                def store(tile, value):
                    out[pl.ds(pl.multiple_of(tile * LANES + first, 8), 8), lanes] = value

                backward_stage(spec, store, 0, 1)
            return carry

        lax.fori_loop(0, LANES // 8, body, 0)


def sky_backward_kernel(spectrum, high, low, out, held):
    rows, width = out.shape
    step = pl.program_id(0)
    for i in range(BATCH):
        held[step * BATCH + i] = multiply(split(spectrum[i]), (high[i], low[i]))

    @pl.when(step == pl.num_programs(0) - 1)
    def _():
        def store(tile, at, value):
            out[at, tile * LANES : (tile + 1) * LANES] = -value

        rows_backward(store, held, rows, width // LANES)


def finish_kernel(ids, base, delivered, out):
    out[...] = base[...]

    def body(slot, carry):
        block = ids[slot]

        @pl.when(block < out.shape[1] // LANES)
        def _():
            at = pl.ds(pl.multiple_of(block * LANES, LANES), LANES)
            out[:, at] = out[:, at] + delivered[slot]

        return carry

    lax.fori_loop(0, delivered.shape[0], body, 0)


def data_forward_kernel(
    pointing, slots, arrived, data, beam, white, loading, high, low, spec_out, proj_out, held, listed, tiles
):
    dets, width = data.shape
    outer = width // LANES
    wanted, block_rows = slots.shape[0], arrived.shape[1]
    step = pl.program_id(0)

    @pl.when(step == 0)
    def _():
        def place(entry, carry):
            at = pl.ds(pl.multiple_of(entry * block_rows, 8), block_rows)
            listed[at, :] = arrived[slots[entry]]
            return carry

        lax.fori_loop(0, wanted, place, 0)
        response = split(beam[...])

        def fetch(tile, carry):
            for det in range(dets):
                tiles[tile, det : det + 1, :] = listed[pl.ds(pointing[det, tile], 1), :]
            return carry

        lax.fori_loop(0, outer, fetch, 0)

        for tile in range(outer):
            signal = multiply(split(tiles[tile]), response, (((1,), (1,)), ((), ())))
            tiles[tile] = data[:, tile * LANES : (tile + 1) * LANES] - signal

        rows_forward(lambda tile, at: tiles[tile, at, :], held, dets, outer)

    for i in range(BATCH):
        group = step * BATCH + i
        spec = multiply(split(held[group]), (high[i], low[i]))
        spec_out[i] = spec
        weighted = white[jnp.minimum(group, 1)] * spec
        proj_out[i] = multiply(split(loading[...]), split(weighted), (((0,), (0,)), ((), ())))


def data_backward_kernel(
    pointing, slots, spec, proj, coupling, beam, white, loading, high, low, out, held, tiles, first, second, third, fourth
):
    dets = spec.shape[1]
    modes = proj.shape[1]
    outer = tiles.shape[0]
    wanted, block_rows = slots.shape[0], out.shape[1]
    step = pl.program_id(0)
    for i in range(BATCH):
        group = step * BATCH + i
        kind = jnp.minimum(group, 1)
        coupled = coupling[kind, 0] * proj[i, 0:1, :]
        for mode in range(1, modes):
            coupled = coupled + coupling[kind, mode] * proj[i, mode : mode + 1, :]
        common = multiply(split(loading[...]), split(coupled))
        filtered = white[kind] * (spec[i] - common)
        held[group] = multiply(split(filtered), (high[i], low[i]))

    @pl.when(step == pl.num_programs(0) - 1)
    def _():
        def store(tile, at, value):
            tiles[tile, at, :] = value

        rows_backward(store, held, dets, outer)
        sums = (first, second, third, fourth)
        for total in sums:
            total[...] = jnp.zeros_like(total)
        out[...] = jnp.zeros_like(out)
        response = split(beam[...])
        for tile in range(outer):
            tiles[tile] = multiply(split(tiles[tile]), response)

        def add(tile, carry):
            for det in range(dets):
                total = sums[det % 4]
                at = pl.ds(pointing[det, tile], 1)
                total[at, :] = total[at, :] + tiles[tile, det : det + 1, :]
            return carry

        lax.fori_loop(0, outer, add, 0)

        def place(entry, carry):
            at = pl.ds(pl.multiple_of(entry * block_rows, 8), block_rows)
            out[slots[entry]] = (first[at, :] + second[at, :]) + (third[at, :] + fourth[at, :])
            return carry

        lax.fori_loop(0, wanted, place, 0)


SCALARS = pl.BlockSpec(memory_space=pltpu.SMEM)


def whole(array):
    return pl.BlockSpec(array.shape, lambda g, n=len(array.shape): (0,) * n)


def sliced(array):
    return pl.BlockSpec((BATCH,) + array.shape[1:], lambda g, n=len(array.shape): (g,) + (0,) * (n - 1))


PARAMS = pltpu.CompilerParams(vmem_limit_bytes=LIMIT)


def struct(*shape):
    return jax.ShapeDtypeStruct(shape, F32)


def local(
    detector_data,
    sky_map,
    pointing,
    request_owner,
    request_block,
    beam_kernel,
    inv_white,
    mode_loading,
    mode_kernel,
):
    dets, samples = detector_data.shape
    rows_here, map_cols = sky_map.shape
    owners = lax.axis_size("tm")
    devices = lax.axis_size("det") * owners
    tile = beam_kernel.shape[0]
    blocks_here = map_cols // tile
    wanted = request_owner.shape[0]
    capacity = max(2, 2 * wanted // owners)
    slots = owners * capacity
    modes = mode_loading.shape[1]
    bands = inv_white.shape[1]
    per_device = map_cols // devices
    total_rows = rows_here * devices
    wide = 2 * LANES

    row_forward, row_backward = [halves(t) for t in group_tables(map_cols)]
    row_forward = [jnp.asarray(t) for t in row_forward]
    row_backward = [jnp.asarray(t) for t in row_backward]
    if samples == map_cols:
        time_forward, time_backward = row_forward, row_backward
    else:
        time_forward, time_backward = [[jnp.asarray(h) for h in halves(t)] for t in group_tables(samples)]
    col_f, col_b = group_tables(total_rows)
    col_forward = [jnp.asarray(t) for t in halves(col_f.transpose(0, 2, 1))]
    col_backward = [jnp.asarray(t) for t in halves(col_b.transpose(0, 2, 1))]
    groups = map_cols // LANES // 2
    time_groups = samples // LANES // 2
    col_groups = total_rows // LANES // 2

    target = request_owner[:, 0]
    entry = jnp.arange(wanted, dtype=jnp.int32)
    earlier = (target[:, None] == target[None, :]) & (entry[None, :] < entry[:, None])
    slot_index = target * capacity + jnp.sum(earlier.astype(jnp.int32), axis=1)
    named = slot_index[None, :] == jnp.arange(slots, dtype=jnp.int32)[:, None]
    send_ids = blocks_here + jnp.sum(jnp.where(named, request_block[None, :] - blocks_here, 0), axis=1)
    asked_ids = lax.all_to_all(
        send_ids.reshape(owners, capacity), "tm", split_axis=0, concat_axis=0, tiled=True
    ).reshape(-1)

    packed = pl.pallas_call(
        sky_forward_kernel,
        grid=(groups // BATCH,),
        in_specs=[whole(sky_map), sliced(row_forward[0]), sliced(row_forward[1])],
        out_specs=pl.BlockSpec((BATCH, rows_here, wide), lambda g: (g, 0, 0)),
        out_shape=struct(groups, rows_here, wide),
        scratch_shapes=[pltpu.VMEM((groups, rows_here, wide), F32)],
        compiler_params=PARAMS,
        name="sky_forward",
    )(sky_map, *row_forward)
    parts = wide // per_device
    if parts > 1:
        packed = packed.reshape(groups, rows_here, parts, per_device).transpose(0, 2, 1, 3)
        packed = packed.reshape(devices, rows_here, per_device)
    packed, asked_ids = lax.optimization_barrier((packed, asked_ids))
    columns = lax.all_to_all(packed, ("det", "tm"), split_axis=0, concat_axis=0, tiled=True)
    outgoing = pl.pallas_call(
        pick_kernel,
        in_specs=[SCALARS, pl.BlockSpec(memory_space=pltpu.VMEM)],
        out_specs=pl.BlockSpec(memory_space=pltpu.VMEM),
        out_shape=struct(slots, rows_here, tile),
        compiler_params=PARAMS,
        name="pick_blocks",
    )(asked_ids, sky_map)
    columns, outgoing = lax.optimization_barrier((columns, outgoing))
    columns = columns.reshape(total_rows, per_device)
    arrived = lax.all_to_all(
        outgoing.reshape(owners, capacity, rows_here, tile), "tm", split_axis=0, concat_axis=0, tiled=True
    ).reshape(slots, rows_here, tile)

    rank = lax.axis_index("det") * owners + lax.axis_index("tm")
    col_freq = group_frequencies(map_cols).reshape(-1)
    col_sq = (np.minimum(col_freq, map_cols - col_freq) / map_cols) ** 2
    col_sq = lax.dynamic_slice_in_dim(
        jnp.asarray(col_sq.astype(np.float32).reshape(devices, per_device)), rank, 1, 0
    )
    row_freq = group_frequencies(total_rows)
    row_sq = ((np.minimum(row_freq, total_rows - row_freq) / total_rows) ** 2).astype(np.float32)
    row_sq = jnp.asarray(row_sq[:, :, None])
    knee_sq = 1.0 / (2.0 * math.pi * total_rows / 64.0) ** 2
    backed = pl.pallas_call(
        functools.partial(column_kernel, knee_sq=knee_sq),
        grid=(col_groups // BATCH,),
        in_specs=[whole(columns), sliced(row_sq), whole(col_sq)]
        + [sliced(t) for t in col_forward + col_backward],
        out_specs=pl.BlockSpec((total_rows, per_device), lambda g: (0, 0)),
        out_shape=struct(total_rows, per_device),
        scratch_shapes=[pltpu.VMEM((col_groups, wide, per_device), F32)],
        compiler_params=PARAMS,
        name="sky_columns",
    )(columns, row_sq, col_sq, *col_forward, *col_backward)
    backed, arrived = lax.optimization_barrier((backed, arrived))
    spectrum = lax.all_to_all(
        backed.reshape(devices, rows_here, per_device),
        ("det", "tm"),
        split_axis=0,
        concat_axis=0,
        tiled=True,
    )
    if parts > 1:
        spectrum = spectrum.reshape(groups, parts, rows_here, per_device).transpose(0, 2, 1, 3)
        spectrum = spectrum.reshape(groups, rows_here, wide)

    freq = group_frequencies(samples)[:2]
    band = np.minimum(np.minimum(freq, samples - freq) // BAND_WIDTH, bands - 1)
    onehot = jnp.asarray((np.arange(bands)[:, None, None] == band[None]).astype(np.float32))
    precise = lax.Precision.HIGHEST
    white = jnp.einsum("jb,bgf->gjf", inv_white, onehot, precision=precise)
    coupling = jnp.einsum("bmn,bgf->gnmf", mode_kernel, onehot, precision=precise)
    spec, proj = pl.pallas_call(
        data_forward_kernel,
        grid=(time_groups // BATCH,),
        in_specs=[
            SCALARS,
            SCALARS,
            whole(arrived),
            whole(detector_data),
            whole(beam_kernel),
            whole(white),
            whole(mode_loading),
            sliced(time_forward[0]),
            sliced(time_forward[1]),
        ],
        out_specs=[
            pl.BlockSpec((BATCH, dets, wide), lambda g: (g, 0, 0)),
            pl.BlockSpec((BATCH, modes, wide), lambda g: (g, 0, 0)),
        ],
        out_shape=[struct(time_groups, dets, wide), struct(time_groups, modes, wide)],
        scratch_shapes=[
            pltpu.VMEM((time_groups, dets, wide), F32),
            pltpu.VMEM((wanted * rows_here, tile), F32),
            pltpu.VMEM((samples // tile, dets, tile), F32),
        ],
        compiler_params=PARAMS,
        name="data_forward",
    )(pointing, slot_index, arrived, detector_data, beam_kernel, white, mode_loading, *time_forward)
    proj = lax.psum(proj, "det")

    returned = pl.pallas_call(
        data_backward_kernel,
        grid=(time_groups // BATCH,),
        in_specs=[
            SCALARS,
            SCALARS,
            sliced(spec),
            sliced(proj),
            whole(coupling),
            whole(beam_kernel),
            whole(white),
            whole(mode_loading),
            sliced(time_backward[0]),
            sliced(time_backward[1]),
        ],
        out_specs=pl.BlockSpec((slots, rows_here, tile), lambda g: (0, 0, 0)),
        out_shape=struct(slots, rows_here, tile),
        scratch_shapes=[
            pltpu.VMEM((time_groups, dets, wide), F32),
            pltpu.VMEM((samples // tile, dets, tile), F32),
        ]
        + [pltpu.VMEM((wanted * rows_here, tile), F32)] * 4,
        compiler_params=PARAMS,
        name="data_backward",
    )(pointing, slot_index, spec, proj, coupling, beam_kernel, white, mode_loading, *time_backward)
    returned, spectrum = lax.optimization_barrier((returned, spectrum))
    delivered = lax.all_to_all(
        returned.reshape(owners, capacity, rows_here, tile), "tm", split_axis=0, concat_axis=0, tiled=True
    ).reshape(slots, rows_here, tile)

    base = pl.pallas_call(
        sky_backward_kernel,
        grid=(groups // BATCH,),
        in_specs=[sliced(spectrum), sliced(row_backward[0]), sliced(row_backward[1])],
        out_specs=pl.BlockSpec((rows_here, map_cols), lambda g: (0, 0)),
        out_shape=struct(rows_here, map_cols),
        scratch_shapes=[pltpu.VMEM((groups, rows_here, wide), F32)],
        compiler_params=PARAMS,
        name="sky_backward",
    )(spectrum, *row_backward)

    chunk = rows_here // 4
    return pl.pallas_call(
        finish_kernel,
        grid=(4,),
        in_specs=[
            SCALARS,
            pl.BlockSpec((chunk, map_cols), lambda g: (g, 0)),
            pl.BlockSpec((slots, chunk, tile), lambda g: (0, g, 0)),
        ],
        out_specs=pl.BlockSpec((chunk, map_cols), lambda g: (g, 0)),
        out_shape=struct(rows_here, map_cols),
        compiler_params=PARAMS,
        name="sky_finish",
    )(asked_ids, base, delivered)


def solution(mesh):
    return jax.shard_map(
        local,
        mesh=mesh,
        in_specs=(
            P("det", "tm"),
            P(("det", "tm"), None),
            P("det", "tm"),
            P(("det", "tm"), None),
            P(("det", "tm")),
            P(),
            P("det", None),
            P("det", None),
            P(),
        ),
        out_specs=P(("det", "tm"), None),
        check_vma=False,
    )
```

```python
import functools
import math

import jax
import jax.numpy as jnp
import ml_dtypes
import numpy as np
from jax import lax
from jax.experimental import pallas as pl
from jax.experimental.pallas import tpu as pltpu
from jax.sharding import PartitionSpec as P

BAND_WIDTH = 128
LANES = 128
BATCH = 4
LIMIT = 50 * 1024 * 1024
F32 = jnp.float32
BF16 = jnp.bfloat16


def group_frequencies(length):
    half = LANES // 2
    outer = length // LANES
    steps = np.arange(LANES)
    freq = np.zeros((outer // 2, 2 * LANES), np.int64)
    for group in range(1, outer // 2):
        freq[group] = np.concatenate([group + outer * steps] * 2)
    low = outer * np.concatenate([np.arange(half + 1), np.arange(1, half)])
    middle = outer // 2 + outer * np.concatenate([np.arange(half)] * 2)
    freq[0] = np.concatenate([low, middle])
    return freq


def group_tables(length):
    half = LANES // 2
    freq = group_frequencies(length)
    groups = freq.shape[0]
    steps = np.arange(LANES)
    forward = np.zeros((groups, 2 * LANES, 2 * LANES))
    weight = np.ones((groups, 2 * LANES))
    angle = 2.0 * math.pi / length
    for group in range(groups):
        turn = (steps[:, None] * freq[group][None, :] % length) * angle
        cosine, sine = np.cos(turn), np.sin(turn)
        if group > 0:
            forward[group, :LANES, :LANES] = cosine[:, :LANES]
            forward[group, LANES:, :LANES] = sine[:, :LANES]
            forward[group, :LANES, LANES:] = -sine[:, LANES:]
            forward[group, LANES:, LANES:] = cosine[:, LANES:]
        else:
            forward[0, :LANES, : half + 1] = cosine[:, : half + 1]
            forward[0, :LANES, half + 1 : LANES] = -sine[:, half + 1 : LANES]
            forward[0, LANES:, LANES : LANES + half] = cosine[:, LANES : LANES + half]
            forward[0, LANES:, LANES + half :] = -sine[:, LANES + half :]
            weight[0, :] = 2.0
            weight[0, 0] = 1.0
            weight[0, half] = 1.0
    backward = (forward * weight[:, None, :] / length).transpose(0, 2, 1)
    return forward, backward


def halves(table):
    high = table.astype(np.float32).astype(ml_dtypes.bfloat16)
    low = (table - high.astype(np.float64)).astype(ml_dtypes.bfloat16)
    return high, low


def split(value):
    high = value.astype(BF16)
    return high, (value - high.astype(F32)).astype(BF16)


def multiply(left, right, dims=(((1,), (0,)), ((), ()))):
    dot = functools.partial(lax.dot_general, dimension_numbers=dims, preferred_element_type=F32)
    if dims[0][0] == (0,):
        return dot(left[0], right[0]) + (dot(left[1], right[0]) + dot(left[0], right[1]))
    rows = left[0].shape[0]
    both = dot(jnp.concatenate(left, axis=0), right[0])
    return both[:rows] + (both[rows:] + dot(left[0], right[1]))


def forward_stage(load, start, step, count):
    if count == 2:
        first, second = load(start), load(start + step)
        return [(first + second, None), (first - second, None)]
    even = forward_stage(load, start, 2 * step, count // 2)
    odd = forward_stage(load, start + step, 2 * step, count // 2)
    out = [None] * (count // 2 + 1)
    out[0] = (even[0][0] + odd[0][0], None)
    out[count // 2] = (even[0][0] - odd[0][0], None)
    out[count // 4] = (even[count // 4][0], -odd[count // 4][0])
    for k in range(1, count // 4):
        cosine, sine = math.cos(2 * math.pi * k / count), math.sin(2 * math.pi * k / count)
        odd_re, odd_im = odd[k]
        turn_re = cosine * odd_re + sine * odd_im
        turn_im = cosine * odd_im - sine * odd_re
        out[k] = (even[k][0] + turn_re, even[k][1] + turn_im)
        out[count // 2 - k] = (even[k][0] - turn_re, turn_im - even[k][1])
    return out


def backward_stage(spec, store, start, step):
    count = 2 * (len(spec) - 1)
    if count == 2:
        store(start, spec[0][0] + spec[1][0])
        store(start + step, spec[0][0] - spec[1][0])
        return
    even, odd = [None] * (count // 4 + 1), [None] * (count // 4 + 1)
    even[0] = (spec[0][0] + spec[count // 2][0], None)
    odd[0] = (spec[0][0] - spec[count // 2][0], None)
    middle = spec[count // 4]
    even[count // 4] = (2.0 * middle[0], None)
    odd[count // 4] = (-2.0 * middle[1], None)
    for k in range(1, count // 4):
        cosine, sine = math.cos(2 * math.pi * k / count), math.sin(2 * math.pi * k / count)
        (a_re, a_im), (b_re, b_im) = spec[k], spec[count // 2 - k]
        even[k] = (a_re + b_re, a_im - b_im)
        diff_re, diff_im = a_re - b_re, a_im + b_im
        odd[k] = (diff_re * cosine - diff_im * sine, diff_re * sine + diff_im * cosine)
    backward_stage(even, store, start, 2 * step)
    backward_stage(odd, store, start + step, 2 * step)


def rows_forward(load_tile, held, rows, outer):
    def body(index, carry):
        at = pl.ds(pl.multiple_of(index * 8, 8), 8)
        spec = forward_stage(lambda tile: load_tile(tile, at), 0, 1, outer)
        held[0, at, :LANES] = spec[0][0]
        held[0, at, LANES:] = spec[outer // 2][0]
        for k in range(1, outer // 2):
            held[k, at, :LANES] = spec[k][0]
            held[k, at, LANES:] = spec[k][1]
        return carry

    lax.fori_loop(0, rows // 8, body, 0)


def rows_backward(store_tile, held, rows, outer):
    def body(index, carry):
        at = pl.ds(pl.multiple_of(index * 8, 8), 8)
        spec = [(held[0, at, :LANES], None)]
        for k in range(1, outer // 2):
            spec.append((held[k, at, :LANES], held[k, at, LANES:]))
        spec.append((held[0, at, LANES:], None))
        backward_stage(spec, lambda tile, value: store_tile(tile, at, value), 0, 1)
        return carry

    lax.fori_loop(0, rows // 8, body, 0)


def pick_kernel(ids, sky, out):
    slots, last = out.shape[0], sky.shape[1] // LANES - 1

    def body(slot, carry):
        at = pl.multiple_of(jnp.minimum(ids[slot], last) * LANES, LANES)
        out[slot] = sky[:, pl.ds(at, LANES)]
        return carry

    lax.fori_loop(0, slots, body, 0)


def sky_forward_kernel(sky, high, low, out, held):
    rows, width = sky.shape
    step = pl.program_id(0)

    @pl.when(step == 0)
    def _():
        def load(tile, at):
            return sky[at, tile * LANES : (tile + 1) * LANES]

        rows_forward(load, held, rows, width // LANES)

    for i in range(BATCH):
        out[i] = multiply(split(held[step * BATCH + i]), (high[i], low[i]))


def column_kernel(cols, row_sq, col_sq, f_high, f_low, b_high, b_low, out, held, *, knee_sq):
    length, width = cols.shape
    outer = length // LANES
    step = pl.program_id(0)
    chunks = [(at, min(LANES, width)) for at in range(0, width, LANES)]

    @pl.when(step == 0)
    def _():
        def body(index, carry):
            first = pl.multiple_of(index * 8, 8)
            near, far = pl.ds(first, 8), pl.ds(pl.multiple_of(first + LANES, 8), 8)
            for start, size in chunks:
                lanes = slice(start, start + size)

                def load(tile):
                    return cols[pl.ds(pl.multiple_of(tile * LANES + first, 8), 8), lanes]

                spec = forward_stage(load, 0, 1, outer)
                held[0, near, lanes] = spec[0][0]
                held[0, far, lanes] = spec[outer // 2][0]
                for k in range(1, outer // 2):
                    held[k, near, lanes] = spec[k][0]
                    held[k, far, lanes] = spec[k][1]
            return carry

        lax.fori_loop(0, LANES // 8, body, 0)

    for i in range(BATCH):
        group = step * BATCH + i
        spectrum = multiply((f_high[i], f_low[i]), split(held[group]))
        radial_sq = row_sq[i] + col_sq[...]
        gain = 1.0 + radial_sq * 20.0 + 0.25 * lax.rsqrt(radial_sq + knee_sq)
        held[group] = multiply((b_high[i], b_low[i]), split(spectrum * gain))

    @pl.when(step == pl.num_programs(0) - 1)
    def _():
        def body(index, carry):
            first = pl.multiple_of(index * 8, 8)
            near, far = pl.ds(first, 8), pl.ds(pl.multiple_of(first + LANES, 8), 8)
            for start, size in chunks:
                lanes = slice(start, start + size)
                spec = [(held[0, near, lanes], None)]
                for k in range(1, outer // 2):
                    spec.append((held[k, near, lanes], held[k, far, lanes]))
                spec.append((held[0, far, lanes], None))

                def store(tile, value):
                    out[pl.ds(pl.multiple_of(tile * LANES + first, 8), 8), lanes] = value

                backward_stage(spec, store, 0, 1)
            return carry

        lax.fori_loop(0, LANES // 8, body, 0)


def sky_backward_kernel(spectrum, high, low, out, held):
    rows, width = out.shape
    step = pl.program_id(0)
    for i in range(BATCH):
        held[step * BATCH + i] = multiply(split(spectrum[i]), (high[i], low[i]))

    @pl.when(step == pl.num_programs(0) - 1)
    def _():
        def store(tile, at, value):
            out[at, tile * LANES : (tile + 1) * LANES] = -value

        rows_backward(store, held, rows, width // LANES)


def finish_kernel(ids, base, delivered, out):
    out[...] = base[...]

    def body(slot, carry):
        block = ids[slot]

        @pl.when(block < out.shape[1] // LANES)
        def _():
            at = pl.ds(pl.multiple_of(block * LANES, LANES), LANES)
            out[:, at] = out[:, at] + delivered[slot]

        return carry

    lax.fori_loop(0, delivered.shape[0], body, 0)


def data_forward_kernel(
    pointing, slots, arrived, data, beam, white, loading, high, low, spec_out, proj_out, held, listed, tiles
):
    dets, width = data.shape
    outer = width // LANES
    wanted, block_rows = slots.shape[0], arrived.shape[1]
    step = pl.program_id(0)

    @pl.when(step == 0)
    def _():
        def place(entry, carry):
            at = pl.ds(pl.multiple_of(entry * block_rows, 8), block_rows)
            listed[at, :] = arrived[slots[entry]]
            return carry

        lax.fori_loop(0, wanted, place, 0)
        response = split(beam[...])

        def fetch(tile, carry):
            for det in range(dets):
                tiles[tile, det : det + 1, :] = listed[pl.ds(pointing[det, tile], 1), :]
            return carry

        lax.fori_loop(0, outer, fetch, 0)

        for tile in range(outer):
            signal = multiply(split(tiles[tile]), response, (((1,), (1,)), ((), ())))
            tiles[tile] = data[:, tile * LANES : (tile + 1) * LANES] - signal

        rows_forward(lambda tile, at: tiles[tile, at, :], held, dets, outer)

    for i in range(BATCH):
        group = step * BATCH + i
        spec = multiply(split(held[group]), (high[i], low[i]))
        spec_out[i] = spec
        weighted = white[jnp.minimum(group, 1)] * spec
        proj_out[i] = multiply(split(loading[...]), split(weighted), (((0,), (0,)), ((), ())))


def data_backward_kernel(
    pointing, slots, spec, proj, coupling, beam, white, loading, high, low, out, held, tiles, first, second, third, fourth
):
    dets = spec.shape[1]
    modes = proj.shape[1]
    outer = tiles.shape[0]
    wanted, block_rows = slots.shape[0], out.shape[1]
    step = pl.program_id(0)
    for i in range(BATCH):
        group = step * BATCH + i
        kind = jnp.minimum(group, 1)
        coupled = coupling[kind, 0] * proj[i, 0:1, :]
        for mode in range(1, modes):
            coupled = coupled + coupling[kind, mode] * proj[i, mode : mode + 1, :]
        common = multiply(split(loading[...]), split(coupled))
        filtered = white[kind] * (spec[i] - common)
        held[group] = multiply(split(filtered), (high[i], low[i]))

    @pl.when(step == pl.num_programs(0) - 1)
    def _():
        def store(tile, at, value):
            tiles[tile, at, :] = value

        rows_backward(store, held, dets, outer)
        sums = (first, second, third, fourth)
        for total in sums:
            total[...] = jnp.zeros_like(total)
        out[...] = jnp.zeros_like(out)
        response = split(beam[...])
        for tile in range(outer):
            tiles[tile] = multiply(split(tiles[tile]), response)

        def add(tile, carry):
            for det in range(dets):
                total = sums[det % 4]
                at = pl.ds(pointing[det, tile], 1)
                total[at, :] = total[at, :] + tiles[tile, det : det + 1, :]
            return carry

        lax.fori_loop(0, outer, add, 0)

        def place(entry, carry):
            at = pl.ds(pl.multiple_of(entry * block_rows, 8), block_rows)
            out[slots[entry]] = (first[at, :] + second[at, :]) + (third[at, :] + fourth[at, :])
            return carry

        lax.fori_loop(0, wanted, place, 0)


SCALARS = pl.BlockSpec(memory_space=pltpu.SMEM)


def whole(array):
    return pl.BlockSpec(array.shape, lambda g, n=len(array.shape): (0,) * n)


def sliced(array):
    return pl.BlockSpec((BATCH,) + array.shape[1:], lambda g, n=len(array.shape): (g,) + (0,) * (n - 1))


PARAMS = pltpu.CompilerParams(vmem_limit_bytes=LIMIT)
SKY_PARAMS = pltpu.CompilerParams(vmem_limit_bytes=LIMIT // 2)


def struct(*shape):
    return jax.ShapeDtypeStruct(shape, F32)


def local(
    detector_data,
    sky_map,
    pointing,
    request_owner,
    request_block,
    beam_kernel,
    inv_white,
    mode_loading,
    mode_kernel,
):
    dets, samples = detector_data.shape
    rows_here, map_cols = sky_map.shape
    owners = lax.axis_size("tm")
    devices = lax.axis_size("det") * owners
    tile = beam_kernel.shape[0]
    blocks_here = map_cols // tile
    wanted = request_owner.shape[0]
    capacity = max(2, 2 * wanted // owners)
    slots = owners * capacity
    modes = mode_loading.shape[1]
    bands = inv_white.shape[1]
    per_device = map_cols // devices
    total_rows = rows_here * devices
    wide = 2 * LANES

    row_forward, row_backward = [halves(t) for t in group_tables(map_cols)]
    row_forward = [jnp.asarray(t) for t in row_forward]
    row_backward = [jnp.asarray(t) for t in row_backward]
    if samples == map_cols:
        time_forward, time_backward = row_forward, row_backward
    else:
        time_forward, time_backward = [[jnp.asarray(h) for h in halves(t)] for t in group_tables(samples)]
    col_f, col_b = group_tables(total_rows)
    col_forward = [jnp.asarray(t) for t in halves(col_f.transpose(0, 2, 1))]
    col_backward = [jnp.asarray(t) for t in halves(col_b.transpose(0, 2, 1))]
    groups = map_cols // LANES // 2
    time_groups = samples // LANES // 2
    col_groups = total_rows // LANES // 2

    target = request_owner[:, 0]
    entry = jnp.arange(wanted, dtype=jnp.int32)
    earlier = (target[:, None] == target[None, :]) & (entry[None, :] < entry[:, None])
    slot_index = target * capacity + jnp.sum(earlier.astype(jnp.int32), axis=1)
    named = slot_index[None, :] == jnp.arange(slots, dtype=jnp.int32)[:, None]
    send_ids = blocks_here + jnp.sum(jnp.where(named, request_block[None, :] - blocks_here, 0), axis=1)
    asked_ids = lax.all_to_all(
        send_ids.reshape(owners, capacity), "tm", split_axis=0, concat_axis=0, tiled=True
    ).reshape(-1)

    packed = pl.pallas_call(
        sky_forward_kernel,
        grid=(groups // BATCH,),
        in_specs=[whole(sky_map), sliced(row_forward[0]), sliced(row_forward[1])],
        out_specs=pl.BlockSpec((BATCH, rows_here, wide), lambda g: (g, 0, 0)),
        out_shape=struct(groups, rows_here, wide),
        scratch_shapes=[pltpu.VMEM((groups, rows_here, wide), F32)],
        compiler_params=SKY_PARAMS,
        name="sky_forward",
    )(sky_map, *row_forward)
    parts = wide // per_device
    if parts > 1:
        packed = packed.reshape(groups, rows_here, parts, per_device).transpose(0, 2, 1, 3)
        packed = packed.reshape(devices, rows_here, per_device)
    packed, asked_ids = lax.optimization_barrier((packed, asked_ids))
    columns = lax.all_to_all(packed, ("det", "tm"), split_axis=0, concat_axis=0, tiled=True)
    outgoing = pl.pallas_call(
        pick_kernel,
        in_specs=[SCALARS, pl.BlockSpec(memory_space=pltpu.VMEM)],
        out_specs=pl.BlockSpec(memory_space=pltpu.VMEM),
        out_shape=struct(slots, rows_here, tile),
        compiler_params=PARAMS,
        name="pick_blocks",
    )(asked_ids, sky_map)
    columns, outgoing = lax.optimization_barrier((columns, outgoing))
    columns = columns.reshape(total_rows, per_device)
    arrived = lax.all_to_all(
        outgoing.reshape(owners, capacity, rows_here, tile), "tm", split_axis=0, concat_axis=0, tiled=True
    ).reshape(slots, rows_here, tile)

    rank = lax.axis_index("det") * owners + lax.axis_index("tm")
    col_freq = group_frequencies(map_cols).reshape(-1)
    col_sq = (np.minimum(col_freq, map_cols - col_freq) / map_cols) ** 2
    col_sq = lax.dynamic_slice_in_dim(
        jnp.asarray(col_sq.astype(np.float32).reshape(devices, per_device)), rank, 1, 0
    )
    row_freq = group_frequencies(total_rows)
    row_sq = ((np.minimum(row_freq, total_rows - row_freq) / total_rows) ** 2).astype(np.float32)
    row_sq = jnp.asarray(row_sq[:, :, None])
    knee_sq = 1.0 / (2.0 * math.pi * total_rows / 64.0) ** 2
    backed = pl.pallas_call(
        functools.partial(column_kernel, knee_sq=knee_sq),
        grid=(col_groups // BATCH,),
        in_specs=[whole(columns), sliced(row_sq), whole(col_sq)]
        + [sliced(t) for t in col_forward + col_backward],
        out_specs=pl.BlockSpec((total_rows, per_device), lambda g: (0, 0)),
        out_shape=struct(total_rows, per_device),
        scratch_shapes=[pltpu.VMEM((col_groups, wide, per_device), F32)],
        compiler_params=PARAMS,
        name="sky_columns",
    )(columns, row_sq, col_sq, *col_forward, *col_backward)
    backed, arrived = lax.optimization_barrier((backed, arrived))
    spectrum = lax.all_to_all(
        backed.reshape(devices, rows_here, per_device),
        ("det", "tm"),
        split_axis=0,
        concat_axis=0,
        tiled=True,
    )
    if parts > 1:
        spectrum = spectrum.reshape(groups, parts, rows_here, per_device).transpose(0, 2, 1, 3)
        spectrum = spectrum.reshape(groups, rows_here, wide)

    freq = group_frequencies(samples)[:2]
    band = np.minimum(np.minimum(freq, samples - freq) // BAND_WIDTH, bands - 1)
    onehot = jnp.asarray((np.arange(bands)[:, None, None] == band[None]).astype(np.float32))
    precise = lax.Precision.HIGHEST
    white = jnp.einsum("jb,bgf->gjf", inv_white, onehot, precision=precise)
    coupling = jnp.einsum("bmn,bgf->gnmf", mode_kernel, onehot, precision=precise)
    spec, proj = pl.pallas_call(
        data_forward_kernel,
        grid=(time_groups // BATCH,),
        in_specs=[
            SCALARS,
            SCALARS,
            whole(arrived),
            whole(detector_data),
            whole(beam_kernel),
            whole(white),
            whole(mode_loading),
            sliced(time_forward[0]),
            sliced(time_forward[1]),
        ],
        out_specs=[
            pl.BlockSpec((BATCH, dets, wide), lambda g: (g, 0, 0)),
            pl.BlockSpec((BATCH, modes, wide), lambda g: (g, 0, 0)),
        ],
        out_shape=[struct(time_groups, dets, wide), struct(time_groups, modes, wide)],
        scratch_shapes=[
            pltpu.VMEM((time_groups, dets, wide), F32),
            pltpu.VMEM((wanted * rows_here, tile), F32),
            pltpu.VMEM((samples // tile, dets, tile), F32),
        ],
        compiler_params=PARAMS,
        name="data_forward",
    )(pointing, slot_index, arrived, detector_data, beam_kernel, white, mode_loading, *time_forward)
    proj = lax.psum(proj, "det")

    returned = pl.pallas_call(
        data_backward_kernel,
        grid=(time_groups // BATCH,),
        in_specs=[
            SCALARS,
            SCALARS,
            sliced(spec),
            sliced(proj),
            whole(coupling),
            whole(beam_kernel),
            whole(white),
            whole(mode_loading),
            sliced(time_backward[0]),
            sliced(time_backward[1]),
        ],
        out_specs=pl.BlockSpec((slots, rows_here, tile), lambda g: (0, 0, 0)),
        out_shape=struct(slots, rows_here, tile),
        scratch_shapes=[
            pltpu.VMEM((time_groups, dets, wide), F32),
            pltpu.VMEM((samples // tile, dets, tile), F32),
        ]
        + [pltpu.VMEM((wanted * rows_here, tile), F32)] * 4,
        compiler_params=PARAMS,
        name="data_backward",
    )(pointing, slot_index, spec, proj, coupling, beam_kernel, white, mode_loading, *time_backward)
    returned, spectrum = lax.optimization_barrier((returned, spectrum))
    delivered = lax.all_to_all(
        returned.reshape(owners, capacity, rows_here, tile), "tm", split_axis=0, concat_axis=0, tiled=True
    ).reshape(slots, rows_here, tile)

    base = pl.pallas_call(
        sky_backward_kernel,
        grid=(groups // BATCH,),
        in_specs=[sliced(spectrum), sliced(row_backward[0]), sliced(row_backward[1])],
        out_specs=pl.BlockSpec((rows_here, map_cols), lambda g: (0, 0)),
        out_shape=struct(rows_here, map_cols),
        scratch_shapes=[pltpu.VMEM((groups, rows_here, wide), F32)],
        compiler_params=SKY_PARAMS,
        name="sky_backward",
    )(spectrum, *row_backward)

    chunk = rows_here // 4
    return pl.pallas_call(
        finish_kernel,
        grid=(4,),
        in_specs=[
            SCALARS,
            pl.BlockSpec((chunk, map_cols), lambda g: (g, 0)),
            pl.BlockSpec((slots, chunk, tile), lambda g: (0, g, 0)),
        ],
        out_specs=pl.BlockSpec((chunk, map_cols), lambda g: (g, 0)),
        out_shape=struct(rows_here, map_cols),
        compiler_params=SKY_PARAMS,
        name="sky_finish",
    )(asked_ids, base, delivered)


def solution(mesh):
    return jax.shard_map(
        local,
        mesh=mesh,
        in_specs=(
            P("det", "tm"),
            P(("det", "tm"), None),
            P("det", "tm"),
            P(("det", "tm"), None),
            P(("det", "tm")),
            P(),
            P("det", None),
            P("det", None),
            P(),
        ),
        out_specs=P(("det", "tm"), None),
        check_vma=False,
    )
```
